32 devices in a mesh: dp: 8 (over z, y), factor: 4 (over x, core).
Axes of the slice: x: 2, y: 2, z: 4, core: 2. Of those that a mesh axis runs over, the one named last changes fastest.
Arguments:
- train_inputs: bfloat16 [64, 8, 64, 320], P('dp'), may hold values from -6 to 6
- train_cotangents: bfloat16 [64, 8, 64, 320], P('dp'), may hold values from -0.26367188 to 0.26367188
- query_inputs: bfloat16 [8, 8, 64, 320], P('dp'), may hold values from -6 to 6
- query_cotangents: bfloat16 [8, 8, 64, 320], P('dp'), may hold values from -0.26367188 to 0.26367188
- timesteps: int32 [64], P('dp'), may hold values from 0 to 999
- input_basis: bfloat16 [2880, 2880], P('dp', 'factor'), may hold values from -0.109375 to 0.109375
- output_basis: bfloat16 [320, 320], replicated, may hold values from -0.3125 to 0.3125
- eigenvalues: float32 [320, 2880], P(None, 'factor'), may hold values from 0.1 to 10
Outputs:
- scores: float32 [64], P('dp')
- query_proj: float32 [320, 2880], P(None, 'factor')
The draws below stay inside these ranges and needn't reach their ends.
All inputs are finite; a program needn't handle non-finite values.
Results may differ from the reference program's by a relative error of at most 0.0037.
Values may be sent and summed in bfloat16 or wider, within the bound.
No kernel may reach another device: no remote copies, remote signals or barrier semaphores. Data moves between devices by JAX's collectives and lax.ppermute only.
A program may use at most 192 MiB of HBM per device.

```python
import math
import jax
import jax.numpy as jnp
from jax import lax

C = 320
K = 2880
IMG_W = 64
ROWS = 8
POSITIONS = 512
TRAIN = 64
QUERIES = 8


def set_ends(values, key, least, high):
    longest = values.shape.index(max(values.shape))
    spots = []
    for shift in (0, 1):
        where = [jax.random.randint(jax.random.fold_in(key, axis), (), 0, length) for axis, length in enumerate(values.shape)]
        where[longest] = (where[longest] + shift) % values.shape[longest]
        spots.append(tuple(where))
    return values.at[spots[0]].set(least).at[spots[1]].set(high)


def levels(key, dims, shards, least, largest):
    level, own = 1.0, jax.random.fold_in(key, 6)
    for axis_at, parts in shards:
        draws = jnp.exp(jax.random.uniform(jax.random.fold_in(own, axis_at), (parts,), jnp.float32, least / len(shards), largest / len(shards)))
        level = level * jnp.repeat(draws, dims[axis_at] // parts).reshape([-1 if axis == axis_at else 1 for axis in range(len(dims))])
    return level


def normal_values(own_key, dims, spread, reach, cuts=(), held_as=jnp.bfloat16):
    array = jax.random.normal(own_key, dims, jnp.float32) * spread
    if len(cuts) > 0:
        array = levels(own_key, dims, cuts, -0.22, 0.18) * array
    return jnp.clip(array, min=-reach, max=reach).astype(held_as)


def setup_inputs(seed: int = 0) -> dict:
    keys = jax.random.split(jax.random.key(seed), 9)
    return {
        "train_inputs": normal_values(keys[0], (TRAIN, ROWS, IMG_W, C), 1.0, 6.0, ((0, 8),)),
        "train_cotangents": normal_values(keys[1], (TRAIN, ROWS, IMG_W, C), (POSITIONS ** -0.5), 0.26367188, ((0, 8),)),
        "query_inputs": normal_values(keys[2], (QUERIES, ROWS, IMG_W, C), 1.0, 6.0, ((0, 8),)),
        "query_cotangents": normal_values(keys[3], (QUERIES, ROWS, IMG_W, C), (POSITIONS ** -0.5), 0.26367188, ((0, 8),)),
        "timesteps": set_ends(jax.random.randint(keys[4], (TRAIN,), 0, 1000), jax.random.fold_in(keys[4], 1), 0, 999).astype(jnp.int32),
        "input_basis": normal_values(keys[5], (K, K), K ** -0.5, 0.109375, ((0, 8), (1, 4))),
        "output_basis": normal_values(keys[6], (C, C), C ** -0.5, 0.3125),
        "eigenvalues": jnp.clip(jnp.exp(math.log(10.0) - 4.6051702 * jax.random.uniform(keys[7], (C, K), jnp.float32) ** levels(keys[7], (C, K), ((1, 4),), -0.2, 0.2)), 0.1, 10.0),
    }


def patch_matrix(activations):
    rows_count, cols_count, channels = activations.shape
    padded = jnp.pad(activations, ((1, 1), (1, 1), (0, 0)))
    taps = [padded[row_off:row_off + rows_count, col_off:col_off + cols_count, :] for row_off in range(3) for col_off in range(3)]
    return jnp.concatenate(taps, axis=-1).reshape(rows_count * cols_count, 9 * channels)

def reference(train_inputs, train_cotangents, query_inputs, query_cotangents, timesteps, input_basis, output_basis, eigenvalues):
    high = lax.Precision.HIGHEST
    basis_in = input_basis.astype(jnp.float32)
    basis_out = output_basis.astype(jnp.float32)
    channels = output_basis.shape[0]
    width = input_basis.shape[0]

    def one_query(pair):
        inputs, cotangents = pair
        patches = patch_matrix(inputs).astype(jnp.float32)
        return jnp.dot(cotangents.reshape(-1, channels).astype(jnp.float32).T, patches, precision=high)
    query_grad = lax.optimization_barrier(jnp.sum(lax.map(one_query, (query_inputs, query_cotangents)), axis=0)) / QUERIES
    query_right = jnp.dot(query_grad, basis_in, precision=high)
    query_proj = jnp.dot(basis_out.T, query_right, precision=high) / (eigenvalues + 0.01)

    def one_train(pair):
        inputs, cotangents = pair
        patches = patch_matrix(inputs).astype(jnp.float32)
        projected = jnp.dot(patches, basis_in, precision=high).astype(jnp.bfloat16)
        rotated = jnp.dot(cotangents.reshape(-1, channels), output_basis, preferred_element_type=jnp.float32).astype(jnp.bfloat16)
        train_proj = jnp.dot(rotated.T, projected, preferred_element_type=jnp.float32)
        return jnp.sum(train_proj * query_proj)
    raw_scores = lax.map(one_train, (train_inputs, train_cotangents))
    phase = (timesteps.astype(jnp.float32) / 1000.0 + 0.008) / 1.008 * (math.pi / 2)
    weight = jnp.sin(phase)
    scores = raw_scores * weight / math.sqrt(channels * width)
    return (scores, query_proj)
```

```python
import functools
import math

import jax
import jax.numpy as jnp
from jax import lax
from jax.experimental import pallas as pl
from jax.experimental.pallas import tpu as pltpu
from jax.sharding import PartitionSpec as P

damping = 0.01
bf16 = jnp.bfloat16
f32 = jnp.float32
first_dims = (((0,), (0,)), ((), ()))
mib = 2**20


def patch_matrix(activations):
    rows, cols, channels = activations.shape
    edge = jnp.zeros((rows, 1, channels), activations.dtype)
    before = jnp.concatenate([edge, activations[:, :-1]], axis=1)
    after = jnp.concatenate([activations[:, 1:], edge], axis=1)
    blank = jnp.zeros((cols, channels), activations.dtype)
    shifted = [
        jnp.concatenate([blank, part.reshape(rows * cols, channels), blank], axis=0)
        for part in (before, activations, after)
    ]
    taps = [
        shifted[col_off][row_off * cols : (row_off + rows) * cols]
        for row_off in range(3)
        for col_off in range(3)
    ]
    return jnp.concatenate(taps, axis=1)


def query_kernel(x_ref, c_ref, basis_ref, out_ref, *, scale):
    queries, rows, cols, channels = x_ref.shape
    blocks, own_rows, wide = out_ref.shape
    depth = 9 * channels // blocks
    total = jnp.zeros((own_rows, 9 * channels), f32)
    for query in range(queries):
        cot = c_ref[query].reshape(rows * cols, channels)
        rotated = jnp.dot(cot, basis_ref[...], preferred_element_type=f32)
        upper = rotated.astype(bf16)
        lower = (rotated - upper.astype(f32)).astype(bf16)
        patches = patch_matrix(x_ref[query])
        total += lax.dot_general(upper, patches, first_dims, preferred_element_type=f32)
        total += lax.dot_general(lower, patches, first_dims, preferred_element_type=f32)
    total = total * scale
    largest = jnp.max(jnp.max(jnp.abs(total), axis=1, keepdims=True), axis=0, keepdims=True)
    power = jnp.ceil(jnp.log(jnp.maximum(largest, 1e-30)) * (1 / math.log(2.0))) - 14.0
    total = total * jnp.exp2(-power)
    for block in range(blocks):
        out_ref[block, :, :depth] = total[:, block * depth : (block + 1) * depth]
        out_ref[block, :, depth:] = jnp.broadcast_to(power, (own_rows, wide - depth))


def query_partial(x, cot, basis, blocks, scale):
    channels = x.shape[-1]
    depth = 9 * channels // blocks
    wide = depth + 128 - depth % 128
    return pl.pallas_call(
        functools.partial(query_kernel, scale=scale),
        out_shape=jax.ShapeDtypeStruct((blocks, basis.shape[1], wide), f32),
        compiler_params=pltpu.CompilerParams(vmem_limit_bytes=32 * mib),
        cost_estimate=pl.CostEstimate(
            flops=4 * x.size * 9 * basis.shape[1], bytes_accessed=4 * x.size, transcendentals=0
        ),
        name="query_gradient",
    )(x, cot, basis)


def train_kernel(x_ref, c_ref, basis_ref, out_ref):
    rows, cols, channels = x_ref.shape[1:]
    blocks, _, _, depth = out_ref.shape
    cot = c_ref[0].reshape(rows * cols, channels)
    rotated = jnp.dot(cot, basis_ref[...], preferred_element_type=f32).astype(bf16)
    grad = lax.dot_general(
        rotated, patch_matrix(x_ref[0]), first_dims, preferred_element_type=f32
    ).astype(bf16)
    for block in range(blocks):
        out_ref[block, 0] = grad[:, block * depth : (block + 1) * depth]


def train_gradients(x, cot, basis, blocks):
    count, rows, cols, channels = x.shape
    depth = 9 * channels // blocks
    spec = pl.BlockSpec((1, rows, cols, channels), lambda i: (i, 0, 0, 0))
    return pl.pallas_call(
        train_kernel,
        grid=(count,),
        in_specs=[spec, spec, pl.BlockSpec((channels, channels), lambda i: (0, 0))],
        out_specs=pl.BlockSpec((blocks, 1, channels, depth), lambda i: (0, i, 0, 0)),
        out_shape=jax.ShapeDtypeStruct((blocks, count, channels, depth), bf16),
        compiler_params=pltpu.CompilerParams(vmem_limit_bytes=32 * mib),
        cost_estimate=pl.CostEstimate(
            flops=2 * x.size * 9 * channels, bytes_accessed=4 * x.size, transcendentals=0
        ),
        name="train_gradients",
    )(x, cot, basis)


def place_pair(scratch, slot, side, mine, other):
    depth = mine.shape[0]

    @pl.when(side == 0)
    def _():
        scratch[slot, :depth] = mine[...]
        scratch[slot, depth:] = other[...]

    @pl.when(side == 1)
    def _():
        scratch[slot, :depth] = other[...]
        scratch[slot, depth:] = mine[...]


def early_kernel(where, *refs, slots):
    grads, pieces, out_ref, basis = refs[:slots], refs[slots : 3 * slots], refs[-2], refs[-1]

    @pl.when(pl.program_id(0) == 0)
    def _():
        for slot in range(slots):
            place_pair(basis, slot, where[0], pieces[2 * slot], pieces[2 * slot + 1])

    count, channels, depth = grads[0].shape[1:]
    total = jnp.zeros((count * channels, out_ref.shape[-1]), f32)
    for slot in range(slots):
        total += jnp.dot(
            grads[slot][0].reshape(count * channels, depth),
            basis[slot],
            preferred_element_type=f32,
        )
    out_ref[...] = total.reshape(out_ref.shape)


def early_products(where, grads, pieces, step):
    blocks, count, channels, depth = grads.shape
    slots = len(pieces) // 2
    half, width = pieces[0].shape
    grad_specs = [
        pl.BlockSpec((1, step, channels, depth), lambda i, at, slot=slot: (at[1 + slot], i, 0, 0))
        for slot in range(slots)
    ]
    piece_specs = [pl.BlockSpec((half, width), lambda i, at: (0, 0))] * (2 * slots)
    return pl.pallas_call(
        functools.partial(early_kernel, slots=slots),
        grid_spec=pltpu.PrefetchScalarGridSpec(
            num_scalar_prefetch=1,
            grid=(count // step,),
            in_specs=grad_specs + piece_specs,
            out_specs=pl.BlockSpec((step, channels, width), lambda i, at: (i, 0, 0)),
            scratch_shapes=[pltpu.VMEM((slots, 2 * half, width), bf16)],
        ),
        out_shape=jax.ShapeDtypeStruct((count, channels, width), f32),
        compiler_params=pltpu.CompilerParams(vmem_limit_bytes=48 * mib),
        cost_estimate=pl.CostEstimate(
            flops=2 * slots * count * channels * depth * width,
            bytes_accessed=4 * count * channels * width,
            transcendentals=0,
        ),
        name="early_products",
    )(where, *([grads] * slots), *pieces)


def final_kernel(where, *refs, blocks, parts):
    grad_ref, early_ref, eigen_ref = refs[:3]
    query_refs = refs[3 : 3 + parts]
    pieces = refs[3 + parts : 3 + parts + 2 * blocks]
    score_ref, proj_ref, basis = refs[-3:]

    @pl.when(pl.program_id(0) == 0)
    def _():
        for slot in range(blocks):
            place_pair(basis, slot, where[0], pieces[2 * slot], pieces[2 * slot + 1])
        for part in range(parts):
            at = where[1 + blocks + part]
            total = jnp.dot(query_refs[part][0], basis[0], preferred_element_type=f32)
            for slot in range(1, blocks):
                total += jnp.dot(query_refs[part][slot], basis[slot], preferred_element_type=f32)
            proj_ref[at] = total / (eigen_ref[at] + damping)

    step, channels, depth = grad_ref.shape[1:]
    width = basis.shape[-1]
    proj = proj_ref[...].reshape(channels, width)
    late = jnp.dot(
        grad_ref[0].reshape(step * channels, depth), basis[blocks - 1], preferred_element_type=f32
    ).reshape(step, channels, width)
    for item in range(step):
        sums = jnp.sum((early_ref[item] + late[item]) * proj, axis=0, keepdims=True)
        total = jnp.sum(sums, axis=1, keepdims=True)
        score_ref[0, item : item + 1, :] = jnp.broadcast_to(total, (1, score_ref.shape[2]))


def final_products(where, grads, early, eigen, queries, pieces, step):
    blocks, count, channels, depth = grads.shape
    parts, own_rows, width = eigen.shape
    half = pieces[0].shape[0]
    whole3 = pl.BlockSpec((parts, own_rows, width), lambda i, at: (0, 0, 0))
    return pl.pallas_call(
        functools.partial(final_kernel, blocks=blocks, parts=parts),
        grid_spec=pltpu.PrefetchScalarGridSpec(
            num_scalar_prefetch=1,
            grid=(count // step,),
            in_specs=[
                pl.BlockSpec((1, step, channels, depth), lambda i, at: (at[blocks], i, 0, 0)),
                pl.BlockSpec((step, channels, width), lambda i, at: (i, 0, 0)),
                whole3,
            ]
            + [pl.BlockSpec((blocks, own_rows, depth), lambda i, at: (0, 0, 0))] * parts
            + [pl.BlockSpec((half, width), lambda i, at: (0, 0))] * (2 * blocks),
            out_specs=[
                pl.BlockSpec((1, step, 128), lambda i, at: (i, 0, 0)),
                whole3,
            ],
            scratch_shapes=[pltpu.VMEM((blocks, 2 * half, width), bf16)],
        ),
        out_shape=[
            jax.ShapeDtypeStruct((count // step, step, 128), f32),
            jax.ShapeDtypeStruct((parts, own_rows, width), f32),
        ],
        compiler_params=pltpu.CompilerParams(vmem_limit_bytes=48 * mib),
        cost_estimate=pl.CostEstimate(
            flops=2 * (count + blocks) * channels * depth * width,
            bytes_accessed=4 * count * channels * width,
            transcendentals=0,
        ),
        name="final_products",
    )(where, grads, early, eigen, *queries, *pieces)


def on_device(
    train_inputs,
    train_cotangents,
    query_inputs,
    query_cotangents,
    timesteps,
    input_basis,
    output_basis,
    eigenvalues,
):
    channels = output_basis.shape[0]
    sides = 2
    shards = lax.axis_size("dp")
    rings = shards // sides
    parts = lax.axis_size("factor")
    width = input_basis.shape[0] * shards
    own_rows = channels // parts
    depth = width // rings
    here = lax.axis_index("dp")
    ring, side = here // sides, here % sides
    part = lax.axis_index("factor")

    def along(array, shift):
        pairs = [
            (r * sides + s, (r + shift) % rings * sides + s)
            for r in range(rings)
            for s in range(sides)
        ]
        return lax.ppermute(array, "dp", pairs)

    def across(array):
        return lax.ppermute(array, "dp", [(d, d ^ 1) for d in range(shards)])

    def flip(array, bit):
        return lax.ppermute(array, "factor", [(p, p ^ bit) for p in range(parts)])

    forward = rings // 2
    backward = rings - 1 - forward
    columns = [input_basis]
    for _ in range(forward):
        columns.append(along(columns[-1], 1))
    last = input_basis
    back = []
    for _ in range(backward):
        last = along(last, -1)
        back.append(last)
    order = [0] + [s for pair in zip(range(1, forward + 1), range(rings - 1, forward, -1)) for s in pair]
    order += [s for s in range(1, rings) if s not in order]
    by_shift = {s: columns[s] for s in range(forward + 1)}
    for s, piece in enumerate(back):
        by_shift[rings - 1 - s] = piece
    pieces = []
    for s in order:
        pieces += [by_shift[s], across(by_shift[s])]

    count = query_inputs.shape[0] * shards
    own_basis = lax.dynamic_slice_in_dim(output_basis, part * own_rows, own_rows, axis=1)
    partial = query_partial(query_inputs, query_cotangents, own_basis, rings, 1.0 / count)
    sent = partial.astype(jnp.float16)

    def block_of(array, shift):
        return lax.dynamic_index_in_dim(array, (ring + shift) % rings, 0, keepdims=False)

    arrived = [block_of(sent, 0)] + [along(block_of(sent, s), s) for s in range(1, rings)]
    total = sum(
        item[:, :depth].astype(f32) * jnp.exp2(item[:, depth : depth + 1].astype(f32))
        for item in arrived
    )
    total = (total + across(total)).astype(bf16)
    stack = jnp.stack([total] + [along(total, s) if s else total for s in order[1:]])
    queries, spots = [stack], [0]
    bit = parts // 2
    while bit:
        queries = queries + [flip(item, bit) for item in queries]
        spots = spots + [spot ^ bit for spot in spots]
        bit //= 2

    grads = train_gradients(train_inputs, train_cotangents, output_basis, rings)
    where = jnp.stack(
        [side] + [(ring - s) % rings for s in order] + [part ^ spot for spot in spots]
    ).astype(jnp.int32)
    batch = train_inputs.shape[0]
    step = 2 if batch % 2 == 0 else 1
    early = early_products(where, grads, pieces[:-2], step)
    eigen = eigenvalues.reshape(parts, own_rows, eigenvalues.shape[1])
    sums, proj = final_products(where, grads, early, eigen, queries, pieces, step)
    query_proj = proj.reshape(eigenvalues.shape)
    partial_scores = sums[:, :, 0].reshape(batch)
    raw_scores = partial_scores
    bit = parts // 2
    while bit:
        raw_scores = raw_scores + flip(raw_scores, bit)
        bit //= 2
    phase = (timesteps.astype(f32) / 1000.0 + 0.008) / 1.008 * (math.pi / 2)
    weight = jnp.sin(phase)
    scores = raw_scores * weight / math.sqrt(channels * width)
    return (scores, query_proj)


def solution(mesh):
    in_specs = (
        P("dp", None, None, None),
        P("dp", None, None, None),
        P("dp", None, None, None),
        P("dp", None, None, None),
        P("dp"),
        P("dp", "factor"),
        P(),
        P(None, "factor"),
    )
    out_specs = (P("dp"), P(None, "factor"))
    return jax.shard_map(
        on_device, mesh=mesh, in_specs=in_specs, out_specs=out_specs, check_vma=False
    )
```

```python
import functools
import math

import jax
import jax.numpy as jnp
from jax import lax
from jax.experimental import pallas as pl
from jax.experimental.pallas import tpu as pltpu
from jax.sharding import PartitionSpec as P

damping = 0.01
levels = 32000.0
bf16 = jnp.bfloat16
f32 = jnp.float32
i16 = jnp.int16
i32 = jnp.int32
first_dims = (((0,), (0,)), ((), ()))
last_dims = (((1,), (1,)), ((), ()))
fence = lax.optimization_barrier
mib = 2**20
in_vmem = pl.BlockSpec(memory_space=pltpu.VMEM)
anywhere = pl.BlockSpec(memory_space=pl.ANY)


def padded(size, unit):
    return size + (-size) % unit


def with_scale(size):
    return size + 128 - size % 128


def cheap(flops=1000):
    return pl.CostEstimate(flops=flops, bytes_accessed=1000, transcendentals=0)


def params():
    return pltpu.CompilerParams(vmem_limit_bytes=24 * mib)


def position(groups, parts):
    me, place = lax.axis_index("dp"), lax.axis_index("factor")
    return me, lax.rem(me, groups), lax.div(place, parts), lax.rem(place, parts)


def power_of(*arrays):
    tops = [jnp.max(jnp.max(jnp.abs(a), axis=1, keepdims=True), axis=0, keepdims=True) for a in arrays]
    largest = functools.reduce(jnp.maximum, tops)
    return jnp.ceil(jnp.log(jnp.maximum(largest, 1e-30)) * (1 / math.log(2.0)))


def encode(array, power):
    return jnp.round(array * (jnp.exp2(-power) * levels)).astype(i32).astype(i16)


def put(ref, at, array, power):
    rows, size = array.shape
    wide = ref.shape[-1]
    marks = jnp.broadcast_to(power, (rows, wide - size)).astype(i32).astype(i16)
    if at is None:
        ref[:, :size] = encode(array, power)
        ref[:, size:] = marks
    else:
        ref[at, :, :size] = encode(array, power)
        ref[at, :, size:] = marks


def decode(sent, size):
    values = sent[:, :size].astype(i32).astype(f32)
    power = sent[:, size : size + 1].astype(i32).astype(f32)
    return values * (jnp.exp2(power) * (1 / levels))


def halves(array):
    upper = array.astype(bf16)
    lower = (array - upper.astype(f32)).astype(bf16)
    return upper, lower


def both_halves(array):
    upper = array.astype(bf16).astype(f32)
    return jnp.concatenate([upper, array - upper], axis=0).astype(bf16)


def shifted_inputs(activations):
    rows, cols, channels = activations.shape
    edge = jnp.zeros((rows, 1, channels), activations.dtype)
    before = jnp.concatenate([edge, activations[:, :-1]], axis=1)
    after = jnp.concatenate([activations[:, 1:], edge], axis=1)
    blank = jnp.zeros((cols, channels), activations.dtype)
    return [
        jnp.concatenate([blank, part.reshape(rows * cols, channels), blank], axis=0)
        for part in (before, activations, after)
    ]


def patch_columns(shifted, rows, cols, start, stop):
    channels = shifted[0].shape[1]
    taps = []
    for tap in range(start // channels, -(-stop // channels)):
        row_off, col_off = divmod(tap, 3)
        low, high = max(start - tap * channels, 0), min(stop - tap * channels, channels)
        taps.append(shifted[col_off][row_off * cols : (row_off + rows) * cols, low:high])
    return jnp.concatenate(taps, axis=1)


def fence_blocks(blocks, near, *others):
    held, rest, others = fence(([b for _, b in blocks], [b for _, b in near], others))
    named = [(spot, b) for (spot, _), b in zip(blocks, held)]
    return named, [(spot, b) for (spot, _), b in zip(near, rest)], *others


def query_kernel(x_ref, c_ref, basis_ref, out, chosen_ref, total, *, groups, parts, own_rows, scale):
    queries, rows, cols, channels = x_ref.shape
    shards, high_rows, depth = total.shape
    _, _, side, part = position(groups, parts)
    span = groups * high_rows
    row_at = lax.broadcasted_iota(i32, (channels, span), 0)
    col_at = lax.broadcasted_iota(i32, (channels, span), 1)
    group, item = lax.div(col_at, high_rows), lax.rem(col_at, high_rows)
    wanted = part * groups * own_rows + group * own_rows + item
    chosen = jnp.where((row_at == wanted) & (item < own_rows), 1.0, 0.0).astype(bf16)
    own_basis = jnp.dot(basis_ref[...], chosen, preferred_element_type=f32).astype(bf16)
    chosen_ref[...] = own_basis

    for value in range(2):

        @pl.when(side == value)
        def _(value=value):
            sums = [jnp.zeros((span, depth), f32) for _ in range(2)]
            for query in range(queries):
                cot = c_ref[query].reshape(rows * cols, channels)
                upper, lower = halves(jnp.dot(cot, own_basis, preferred_element_type=f32))
                shifted = shifted_inputs(x_ref[query])
                for half in range(2):
                    start = (2 * half + value) * depth
                    patches = patch_columns(shifted, rows, cols, start, start + depth)
                    for piece in (upper, lower):
                        sums[half] += lax.dot_general(
                            piece, patches, first_dims, preferred_element_type=f32
                        )
            for half in range(2):
                for group in range(groups):
                    total[half * groups + group] = (
                        sums[half][group * high_rows : (group + 1) * high_rows] * scale
                    )

    power = power_of(*[total[shard] for shard in range(shards)])
    for shard in range(shards):
        put(out, shard, total[shard], power)


def query_partial(x, cot, basis, shards, groups, parts, own_rows, scale):
    channels = x.shape[-1]
    high_rows = padded(own_rows, 8)
    depth = 9 * channels // 4
    return pl.pallas_call(
        functools.partial(
            query_kernel, groups=groups, parts=parts, own_rows=own_rows, scale=scale
        ),
        in_specs=[in_vmem] * 3,
        out_specs=[in_vmem] * 2,
        out_shape=[
            jax.ShapeDtypeStruct((shards, high_rows, with_scale(depth)), i16),
            jax.ShapeDtypeStruct((channels, groups * high_rows), bf16),
        ],
        scratch_shapes=[pltpu.VMEM((shards, high_rows, depth), f32)],
        compiler_params=params(),
        cost_estimate=cheap(),
        name="query_gradient",
    )(x, cot, basis)


def train_kernel(basis_ref, x_ref, c_ref, out_ref, *, parts):
    _, rows, cols, channels = x_ref.shape
    shards, _, high_rows, depth = out_ref.shape
    groups = shards // 2
    _, _, side, _ = position(groups, parts)
    cot = c_ref[0].reshape(rows * cols, channels)
    rotated = jnp.dot(cot, basis_ref[...], preferred_element_type=f32).astype(bf16)
    for value in range(2):

        @pl.when(side == value)
        def _(value=value):
            shifted = shifted_inputs(x_ref[0])
            for half in range(2):
                start = (2 * half + value) * depth
                patches = patch_columns(shifted, rows, cols, start, start + depth)
                grad = lax.dot_general(rotated, patches, first_dims, preferred_element_type=f32)
                for group in range(groups):
                    out_ref[half * groups + group, 0] = grad[
                        group * high_rows : (group + 1) * high_rows
                    ]


def train_gradients(chosen, x, cot, shards, parts, first, count, flops):
    _, rows, cols, channels = x.shape
    high_rows = chosen.shape[1] // (shards // 2)
    depth = 9 * channels // 4
    spec = pl.BlockSpec((1, rows, cols, channels), lambda i: (first + i, 0, 0, 0))
    return pl.pallas_call(
        functools.partial(train_kernel, parts=parts),
        grid=(count,),
        in_specs=[pl.BlockSpec(chosen.shape, lambda i: (0, 0)), spec, spec],
        out_specs=pl.BlockSpec((shards, 1, high_rows, depth), lambda i: (0, i, 0, 0)),
        out_shape=jax.ShapeDtypeStruct((shards, count, high_rows, depth), f32),
        compiler_params=params(),
        cost_estimate=cheap(flops),
        name="train_gradients",
    )(chosen, x, cot)


def merge_kernel(arrived, keep_ref, send_ref):
    total = decode(arrived[0], keep_ref.shape[1])
    for shard in range(1, arrived.shape[0]):
        total += decode(arrived[shard], keep_ref.shape[1])
    keep_ref[...] = total
    put(send_ref, None, total, power_of(total))


def merge(arrived, depth):
    _, high_rows, wide = arrived.shape
    return pl.pallas_call(
        merge_kernel,
        in_specs=[in_vmem],
        out_specs=[in_vmem] * 2,
        out_shape=[
            jax.ShapeDtypeStruct((high_rows, depth), f32),
            jax.ShapeDtypeStruct((high_rows, wide), i16),
        ],
        compiler_params=params(),
        cost_estimate=cheap(),
        name="merge",
    )(arrived)


def project_kernel(own_ref, other_ref, *refs, spots, groups, parts):
    pieces, (out, stacked) = refs[: len(spots)], refs[len(spots) :]
    high_rows, depth = own_ref.shape
    rows = depth * 2 // groups
    _, group, side, _ = position(groups, parts)
    own, other = own_ref[...], decode(other_ref, depth)
    for half, value in enumerate(
        (jnp.where(side == 0, own, other), jnp.where(side == 0, other, own))
    ):
        both = both_halves(value)
        for at in range(groups // 2):
            stacked[half * (groups // 2) + at] = both[:, at * rows : (at + 1) * rows]
    results = [0.0] * parts
    for piece, (row, part, start, stop) in zip(pieces, spots):
        left = stacked[jnp.bitwise_xor(group, row)][:, start:stop]
        results[part] += jnp.dot(left, piece[...], preferred_element_type=f32)
    results = [total[:high_rows] + total[high_rows:] for total in results]
    power = power_of(*results)
    for part in range(parts):
        put(out, part, results[part], power)


def project(own, other, blocks, groups, parts):
    spots = [spot for spot, _ in blocks]
    pieces = [piece for _, piece in blocks]
    high_rows, depth = own.shape
    return pl.pallas_call(
        functools.partial(project_kernel, spots=spots, groups=groups, parts=parts),
        in_specs=[in_vmem] * (2 + len(pieces)),
        out_specs=in_vmem,
        out_shape=jax.ShapeDtypeStruct((parts, high_rows, with_scale(pieces[0].shape[1])), i16),
        scratch_shapes=[pltpu.VMEM((groups, 2 * high_rows, depth * 2 // groups), bf16)],
        compiler_params=params(),
        cost_estimate=cheap(),
        name="project",
    )(own, other, *pieces)


def back_kernel(own_ref, other_ref, *refs, spots, groups, parts):
    eigen, refs = refs[:parts], refs[parts:]
    pieces, refs = refs[: len(spots)], refs[len(spots) :]
    proj_ref, keep_ref, send_ref, ordered = refs
    high_rows, width = eigen[0].shape
    _, group, side, _ = position(groups, parts)
    results, stacked = [], []
    for part in range(parts):
        total = decode(own_ref[part], width) + decode(other_ref[part], width)
        results.append(total / (eigen[part][...] + damping))
        stacked.append(both_halves(results[part]))
    sums = {}
    for piece, (row, part, start, stop) in zip(pieces, spots):
        total = lax.dot_general(
            stacked[part], piece[...], last_dims, preferred_element_type=f32
        )
        sums[row, start, stop] = sums.get((row, start, stop), 0.0) + total
    for (row, start, stop), total in sums.items():
        ordered[jnp.bitwise_xor(group, row), :, start:stop] = total[:high_rows] + total[high_rows:]
    sides = [
        jnp.concatenate(
            [ordered[half * (groups // 2) + at] for at in range(groups // 2)], axis=1
        )
        for half in range(2)
    ]
    keep = jnp.where(side == 0, sides[0], sides[1])
    send = jnp.where(side == 0, sides[1], sides[0])
    power = power_of(keep, send)
    put(keep_ref, None, keep, power)
    put(send_ref, None, send, power)
    power = power_of(*results)
    for part in range(parts):
        put(proj_ref, part, results[part], power)


def project_back(own, other, eigen, blocks, rows, groups, parts):
    spots = [spot for spot, _ in blocks]
    pieces = [piece for _, piece in blocks]
    high_rows = eigen[0].shape[0]
    half = jax.ShapeDtypeStruct((high_rows, with_scale(groups * rows // 2)), i16)
    return pl.pallas_call(
        functools.partial(back_kernel, spots=spots, groups=groups, parts=parts),
        in_specs=[in_vmem] * (2 + parts + len(pieces)),
        out_specs=[in_vmem] * 3,
        out_shape=[jax.ShapeDtypeStruct(own.shape, i16), half, half],
        scratch_shapes=[pltpu.VMEM((groups, high_rows, rows), f32)],
        compiler_params=params(),
        cost_estimate=cheap(),
        name="project_back",
    )(own, other, *eigen, *pieces)


def score_kernel(even_ref, odd_ref, *refs):
    grads, out = refs[:-1], refs[-1]
    pairs = even_ref.shape[0]
    count, high_rows, depth = grads[0].shape[1:]
    me = lax.axis_index("dp")
    blocks = []
    for away in range(2 * pairs):
        values = (odd_ref if away % 2 else even_ref)[away // 2]
        blocks.append((jnp.bitwise_xor(me, away), decode(values, depth)))
    for chunk, grad in enumerate(grads):
        for item in range(count):
            total = jnp.zeros((high_rows, depth), f32)
            for at, values in blocks:
                total += grad[at, item] * values
            total = jnp.sum(jnp.sum(total, axis=0, keepdims=True), axis=1, keepdims=True)
            at = chunk * count + item
            out[at : at + 1, :] = jnp.broadcast_to(total, (1, out.shape[1]))


def score_products(even, odd, grads):
    return pl.pallas_call(
        score_kernel,
        in_specs=[in_vmem] * (2 + len(grads)),
        out_specs=in_vmem,
        out_shape=jax.ShapeDtypeStruct((len(grads) * grads[0].shape[1], 128), f32),
        compiler_params=params(),
        cost_estimate=cheap(),
        name="score_products",
    )(even, odd, *grads)


def output_kernel(*refs):
    found, out = refs[:-1], refs[-1]
    parts, groups, own_rows, jump = out.shape
    _, group, _, part = position(groups, parts)
    for pair in range(groups // 2):
        for odd in range(2):
            for away in range(parts):
                value = decode(found[pair][odd, away], jump)
                row = jnp.bitwise_xor(group, 2 * pair + odd)
                out[jnp.bitwise_xor(part, away), row] = value[:own_rows]


def output_rows(found, groups, parts, own_rows, jump):
    return pl.pallas_call(
        output_kernel,
        in_specs=[in_vmem] * len(found),
        out_specs=in_vmem,
        out_shape=jax.ShapeDtypeStruct((parts, groups, own_rows, jump), f32),
        compiler_params=params(),
        cost_estimate=cheap(),
        name="output_rows",
    )(*found)


def on_device(
    train_inputs,
    train_cotangents,
    query_inputs,
    query_cotangents,
    timesteps,
    input_basis,
    output_basis,
    eigenvalues,
):
    channels = output_basis.shape[0]
    shards = lax.axis_size("dp")
    factor = lax.axis_size("factor")
    groups, parts = shards // 2, factor // 2
    width = input_basis.shape[0] * shards
    depth = width // 4
    own_rows = channels // (groups * parts)
    high_rows = padded(own_rows, 8)
    jump = input_basis.shape[1]
    group, part = lax.axis_index("dp") % groups, lax.axis_index("factor") % parts
    early, late = 10**3, 10**10
    batch = train_inputs.shape[0]
    chunks = 2 if batch % 2 == 0 else 1
    rows = input_basis.shape[0]
    cut = padded(rows // 2, 16)

    def swap(array, away):
        return lax.ppermute(array, "dp", [(d, d ^ away) for d in range(shards)])

    def flip(array, away):
        return lax.ppermute(array, "factor", [(p, p ^ away) for p in range(factor)])

    def train(chunk, chosen):
        size = batch // chunks
        return train_gradients(
            chosen, train_inputs, train_cotangents, shards, parts, chunk * size, size, late if chunk else early
        )

    blocks = [((0, 0, 0, rows), input_basis)]
    for away in range(1, groups):
        if away != 3:
            blocks.append(((away, 0, 0, rows), swap(input_basis, away)))
    near = [((0, away, 0, rows), flip(input_basis, away)) for away in range(1, parts)]
    count = query_inputs.shape[0] * shards
    partial, chosen = query_partial(
        query_inputs, query_cotangents, output_basis, shards, groups, parts, own_rows, 1.0 / count
    )
    arrived = lax.all_to_all(partial, "dp", 0, 0)
    trained = [train(0, chosen)]
    blocks, near, trained, chosen = fence_blocks(blocks, near, trained, chosen)

    if groups > 3:
        blocks.append(((3, 0, 0, cut), swap(blocks[2][1][:cut], 1)))
        blocks.append(((3, 0, cut, rows), swap(blocks[1][1][cut:], 2)))
    trained += [train(chunk, chosen) for chunk in range(1, chunks)]
    eigen = []
    for away in range(parts):
        start = ((part ^ away) * groups + group) * own_rows
        lines = lax.dynamic_slice_in_dim(eigenvalues, start, own_rows, axis=0)
        if high_rows > own_rows:
            lines = jnp.pad(lines, ((0, high_rows - own_rows), (0, 0)), constant_values=1.0)
        eigen.append(flip(lines, away) if away else lines)
    blocks, near, trained, arrived, eigen = fence_blocks(blocks, near, trained, arrived, eigen)

    total, sent = merge(arrived, depth)
    other = flip(sent, parts)
    for away in range(1, parts):
        for (row, _, start, stop), piece in blocks[1:]:
            near.append(((row, away, start, stop), flip(piece, away)))
    blocks, near, total, other = fence_blocks(blocks, near, total, other)
    blocks = blocks + near

    own = project(total, other, blocks, groups, parts)
    other = swap(own, groups)
    own, other, eigen = fence((own, other, eigen))

    proj, keep, send = project_back(own, other, eigen, blocks, rows, groups, parts)
    other = flip(send, parts)
    mine = [proj[0]] + [flip(proj[away], away) for away in range(1, parts)]
    keep, other, mine = fence((keep, other, mine))

    power_keep = keep[:, depth : depth + 1].astype(f32)
    power_other = other[:, depth : depth + 1].astype(f32)
    power = jnp.maximum(power_keep, power_other) + 1.0
    values = keep.astype(f32) * jnp.exp2(power_keep - power)
    values += other.astype(f32) * jnp.exp2(power_other - power)
    marked = lax.broadcasted_iota(i32, keep.shape, 1) >= depth
    whole = jnp.where(marked, power, jnp.round(values)).astype(i16)
    even = [whole] + [swap(whole, away) for away in range(2, shards, 2)]
    mine = jnp.stack(mine)
    pair = [mine, swap(mine, 1)]
    even, pair = fence((even, pair))

    even, pair = jnp.stack(even), jnp.stack(pair)
    odd = swap(even, 1)
    found = [pair] + [swap(pair, away) for away in range(2, groups, 2)]
    even, odd, found = fence((even, odd, found))

    sums = score_products(even, odd, trained)
    terms = [sums[:, 0]]
    terms += [flip(terms[0], away) for away in range(1, factor)]
    while len(terms) > 1:
        terms = [terms[at] + terms[at + 1] for at in range(0, len(terms), 2)]
    raw_scores = terms[0]
    query_proj = output_rows(found, groups, parts, own_rows, jump).reshape(channels, jump)
    phase = (timesteps.astype(f32) / 1000.0 + 0.008) / 1.008 * (math.pi / 2)
    weight = jnp.sin(phase)
    scores = raw_scores * weight / math.sqrt(channels * width)
    return (scores, query_proj)


def solution(mesh):
    in_specs = (
        P("dp", None, None, None),
        P("dp", None, None, None),
        P("dp", None, None, None),
        P("dp", None, None, None),
        P("dp"),
        P("dp", "factor"),
        P(),
        P(None, "factor"),
    )
    out_specs = (P("dp"), P(None, "factor"))
    return jax.shard_map(
        on_device, mesh=mesh, in_specs=in_specs, out_specs=out_specs, check_vma=False
    )
```

```python
import functools
import math

import jax
import jax.numpy as jnp
from jax import lax
from jax.experimental import pallas as pl
from jax.experimental.pallas import tpu as pltpu
from jax.sharding import PartitionSpec as P

damping = 0.01
levels = 32000.0
bf16 = jnp.bfloat16
f32 = jnp.float32
i16 = jnp.int16
i32 = jnp.int32
first_dims = (((0,), (0,)), ((), ()))
last_dims = (((1,), (1,)), ((), ()))
fence = lax.optimization_barrier
mib = 2**20
in_vmem = pl.BlockSpec(memory_space=pltpu.VMEM)
anywhere = pl.BlockSpec(memory_space=pl.ANY)


def in_space(array, space):
    return pltpu.with_memory_space_constraint(array, space)


def in_hbm(array):
    return in_space(array, pltpu.HBM)


def padded(size, unit):
    return size + (-size) % unit


def with_scale(size):
    return size + 128 - size % 128


def cheap(flops=1000):
    return pl.CostEstimate(flops=flops, bytes_accessed=1000, transcendentals=0)


def params():
    return pltpu.CompilerParams(vmem_limit_bytes=24 * mib)


def position(groups, parts):
    me, place = lax.axis_index("dp"), lax.axis_index("factor")
    return me, lax.rem(me, groups), lax.div(place, parts), lax.rem(place, parts)


def power_of(*arrays):
    tops = [jnp.max(jnp.max(jnp.abs(a), axis=1, keepdims=True), axis=0, keepdims=True) for a in arrays]
    largest = functools.reduce(jnp.maximum, tops)
    return jnp.ceil(jnp.log(jnp.maximum(largest, 1e-30)) * (1 / math.log(2.0)))


def encode(array, power):
    return jnp.round(array * (jnp.exp2(-power) * levels)).astype(i32).astype(i16)


def put(ref, at, array, power):
    rows, size = array.shape
    wide = ref.shape[-1]
    marks = jnp.broadcast_to(power, (rows, wide - size)).astype(i32).astype(i16)
    if at is None:
        ref[:, :size] = encode(array, power)
        ref[:, size:] = marks
    else:
        ref[at, :, :size] = encode(array, power)
        ref[at, :, size:] = marks


def decode(sent, size):
    values = sent[:, :size].astype(i32).astype(f32)
    power = sent[:, size : size + 1].astype(i32).astype(f32)
    return values * (jnp.exp2(power) * (1 / levels))


def halves(array):
    upper = array.astype(bf16)
    lower = (array - upper.astype(f32)).astype(bf16)
    return upper, lower


def both_halves(array):
    upper = array.astype(bf16).astype(f32)
    return jnp.concatenate([upper, array - upper], axis=0).astype(bf16)


def shifted_inputs(activations):
    rows, cols, channels = activations.shape
    edge = jnp.zeros((rows, 1, channels), activations.dtype)
    before = jnp.concatenate([edge, activations[:, :-1]], axis=1)
    after = jnp.concatenate([activations[:, 1:], edge], axis=1)
    blank = jnp.zeros((cols, channels), activations.dtype)
    return [
        jnp.concatenate([blank, part.reshape(rows * cols, channels), blank], axis=0)
        for part in (before, activations, after)
    ]


def patch_columns(shifted, rows, cols, start, stop):
    channels = shifted[0].shape[1]
    taps = []
    for tap in range(start // channels, -(-stop // channels)):
        row_off, col_off = divmod(tap, 3)
        low, high = max(start - tap * channels, 0), min(stop - tap * channels, channels)
        taps.append(shifted[col_off][row_off * cols : (row_off + rows) * cols, low:high])
    return jnp.concatenate(taps, axis=1)


def fence_blocks(blocks, near, *others):
    held, rest, others = fence(([b for _, b in blocks], [b for _, b in near], others))
    named = [(spot, b) for (spot, _), b in zip(blocks, held)]
    return named, [(spot, b) for (spot, _), b in zip(near, rest)], *others


def query_kernel(x_ref, c_ref, basis_ref, out, chosen_ref, total, *, groups, parts, own_rows, scale):
    queries, rows, cols, channels = x_ref.shape
    shards, high_rows, depth = total.shape
    _, _, side, part = position(groups, parts)
    span = groups * high_rows
    row_at = lax.broadcasted_iota(i32, (channels, span), 0)
    col_at = lax.broadcasted_iota(i32, (channels, span), 1)
    group, item = lax.div(col_at, high_rows), lax.rem(col_at, high_rows)
    wanted = part * groups * own_rows + group * own_rows + item
    chosen = jnp.where((row_at == wanted) & (item < own_rows), 1.0, 0.0).astype(bf16)
    own_basis = jnp.dot(basis_ref[...], chosen, preferred_element_type=f32).astype(bf16)
    chosen_ref[...] = own_basis

    for value in range(2):

        @pl.when(side == value)
        def _(value=value):
            sums = [jnp.zeros((span, depth), f32) for _ in range(2)]
            for query in range(queries):
                cot = c_ref[query].reshape(rows * cols, channels)
                upper, lower = halves(jnp.dot(cot, own_basis, preferred_element_type=f32))
                shifted = shifted_inputs(x_ref[query])
                for half in range(2):
                    start = (2 * half + value) * depth
                    patches = patch_columns(shifted, rows, cols, start, start + depth)
                    for piece in (upper, lower):
                        sums[half] += lax.dot_general(
                            piece, patches, first_dims, preferred_element_type=f32
                        )
            for half in range(2):
                for group in range(groups):
                    total[half * groups + group] = (
                        sums[half][group * high_rows : (group + 1) * high_rows] * scale
                    )

    power = power_of(*[total[shard] for shard in range(shards)])
    for shard in range(shards):
        put(out, shard, total[shard], power)


def query_partial(x, cot, basis, shards, groups, parts, own_rows, scale):
    channels = x.shape[-1]
    high_rows = padded(own_rows, 8)
    depth = 9 * channels // 4
    return pl.pallas_call(
        functools.partial(
            query_kernel, groups=groups, parts=parts, own_rows=own_rows, scale=scale
        ),
        in_specs=[in_vmem] * 3,
        out_specs=[in_vmem] * 2,
        out_shape=[
            jax.ShapeDtypeStruct((shards, high_rows, with_scale(depth)), i16),
            jax.ShapeDtypeStruct((channels, groups * high_rows), bf16),
        ],
        scratch_shapes=[pltpu.VMEM((shards, high_rows, depth), f32)],
        compiler_params=params(),
        cost_estimate=cheap(),
        name="query_gradient",
    )(in_hbm(x), in_hbm(cot), in_hbm(basis))


def train_kernel(basis_ref, x_ref, c_ref, out_ref, *, parts):
    _, rows, cols, channels = x_ref.shape
    shards, _, high_rows, depth = out_ref.shape
    groups = shards // 2
    _, _, side, _ = position(groups, parts)
    cot = c_ref[0].reshape(rows * cols, channels)
    rotated = jnp.dot(cot, basis_ref[...], preferred_element_type=f32).astype(bf16)
    for value in range(2):

        @pl.when(side == value)
        def _(value=value):
            shifted = shifted_inputs(x_ref[0])
            for half in range(2):
                start = (2 * half + value) * depth
                patches = patch_columns(shifted, rows, cols, start, start + depth)
                grad = lax.dot_general(rotated, patches, first_dims, preferred_element_type=f32)
                for group in range(groups):
                    out_ref[half * groups + group, 0] = grad[
                        group * high_rows : (group + 1) * high_rows
                    ]


def train_gradients(chosen, x, cot, shards, parts, first, count, flops):
    _, rows, cols, channels = x.shape
    high_rows = chosen.shape[1] // (shards // 2)
    depth = 9 * channels // 4
    spec = pl.BlockSpec((1, rows, cols, channels), lambda i: (first + i, 0, 0, 0))
    return pl.pallas_call(
        functools.partial(train_kernel, parts=parts),
        grid=(count,),
        in_specs=[pl.BlockSpec(chosen.shape, lambda i: (0, 0)), spec, spec],
        out_specs=pl.BlockSpec((shards, 1, high_rows, depth), lambda i: (0, i, 0, 0)),
        out_shape=pltpu.HBM((shards, count, high_rows, depth), f32),
        compiler_params=params(),
        cost_estimate=cheap(flops),
        name="train_gradients",
    )(chosen, in_hbm(x), in_hbm(cot))


def merge_kernel(arrived, keep_ref, send_ref):
    total = decode(arrived[0], keep_ref.shape[1])
    for shard in range(1, arrived.shape[0]):
        total += decode(arrived[shard], keep_ref.shape[1])
    keep_ref[...] = total
    put(send_ref, None, total, power_of(total))


def merge(arrived, depth):
    _, high_rows, wide = arrived.shape
    return pl.pallas_call(
        merge_kernel,
        in_specs=[in_vmem],
        out_specs=[in_vmem] * 2,
        out_shape=[
            jax.ShapeDtypeStruct((high_rows, depth), f32),
            jax.ShapeDtypeStruct((high_rows, wide), i16),
        ],
        compiler_params=params(),
        cost_estimate=cheap(),
        name="merge",
    )(arrived)


def project_kernel(own_ref, other_ref, *refs, spots, groups, parts):
    pieces, (out, stacked) = refs[: len(spots)], refs[len(spots) :]
    high_rows, depth = own_ref.shape
    rows = depth * 2 // groups
    _, group, side, _ = position(groups, parts)
    own, other = own_ref[...], decode(other_ref, depth)
    for half, value in enumerate(
        (jnp.where(side == 0, own, other), jnp.where(side == 0, other, own))
    ):
        both = both_halves(value)
        for at in range(groups // 2):
            stacked[half * (groups // 2) + at] = both[:, at * rows : (at + 1) * rows]
    results = [0.0] * parts
    for piece, (row, part, start, stop) in zip(pieces, spots):
        left = stacked[jnp.bitwise_xor(group, row)][:, start:stop]
        results[part] += jnp.dot(left, piece[...], preferred_element_type=f32)
    results = [total[:high_rows] + total[high_rows:] for total in results]
    power = power_of(*results)
    for part in range(parts):
        put(out, part, results[part], power)


def project(own, other, blocks, groups, parts):
    spots = [spot for spot, _ in blocks]
    pieces = [piece for _, piece in blocks]
    high_rows, depth = own.shape
    return pl.pallas_call(
        functools.partial(project_kernel, spots=spots, groups=groups, parts=parts),
        in_specs=[in_vmem] * (2 + len(pieces)),
        out_specs=in_vmem,
        out_shape=jax.ShapeDtypeStruct((parts, high_rows, with_scale(pieces[0].shape[1])), i16),
        scratch_shapes=[pltpu.VMEM((groups, 2 * high_rows, depth * 2 // groups), bf16)],
        compiler_params=params(),
        cost_estimate=cheap(),
        name="project",
    )(own, other, *pieces)


def back_kernel(own_ref, other_ref, *refs, spots, groups, parts):
    eigen, refs = refs[:parts], refs[parts:]
    pieces, refs = refs[: len(spots)], refs[len(spots) :]
    proj_ref, keep_ref, send_ref, ordered = refs
    high_rows, width = eigen[0].shape
    _, group, side, _ = position(groups, parts)
    results, stacked = [], []
    for part in range(parts):
        total = decode(own_ref[part], width) + decode(other_ref[part], width)
        results.append(total / (eigen[part][...] + damping))
        stacked.append(both_halves(results[part]))
    sums = {}
    for piece, (row, part, start, stop) in zip(pieces, spots):
        total = lax.dot_general(
            stacked[part], piece[...], last_dims, preferred_element_type=f32
        )
        sums[row, start, stop] = sums.get((row, start, stop), 0.0) + total
    for (row, start, stop), total in sums.items():
        ordered[jnp.bitwise_xor(group, row), :, start:stop] = total[:high_rows] + total[high_rows:]
    sides = [
        jnp.concatenate(
            [ordered[half * (groups // 2) + at] for at in range(groups // 2)], axis=1
        )
        for half in range(2)
    ]
    keep = jnp.where(side == 0, sides[0], sides[1])
    send = jnp.where(side == 0, sides[1], sides[0])
    power = power_of(keep, send)
    put(keep_ref, None, keep, power)
    put(send_ref, None, send, power)
    power = power_of(*results)
    for part in range(parts):
        put(proj_ref, part, results[part], power)


def project_back(own, other, eigen, blocks, rows, groups, parts):
    spots = [spot for spot, _ in blocks]
    pieces = [piece for _, piece in blocks]
    high_rows = eigen[0].shape[0]
    half = jax.ShapeDtypeStruct((high_rows, with_scale(groups * rows // 2)), i16)
    return pl.pallas_call(
        functools.partial(back_kernel, spots=spots, groups=groups, parts=parts),
        in_specs=[in_vmem] * (2 + parts + len(pieces)),
        out_specs=[in_vmem] * 3,
        out_shape=[jax.ShapeDtypeStruct(own.shape, i16), half, half],
        scratch_shapes=[pltpu.VMEM((groups, high_rows, rows), f32)],
        compiler_params=params(),
        cost_estimate=cheap(),
        name="project_back",
    )(own, other, *eigen, *pieces)


def score_kernel(even_ref, odd_ref, *refs):
    grads, out = refs[:-1], refs[-1]
    pairs = even_ref.shape[0]
    count, high_rows, depth = grads[0].shape[1:]
    me = lax.axis_index("dp")
    blocks = []
    for away in range(2 * pairs):
        values = (odd_ref if away % 2 else even_ref)[away // 2]
        blocks.append((jnp.bitwise_xor(me, away), decode(values, depth)))
    for chunk, grad in enumerate(grads):
        for item in range(count):
            total = jnp.zeros((high_rows, depth), f32)
            for at, values in blocks:
                total += grad[at, item] * values
            total = jnp.sum(jnp.sum(total, axis=0, keepdims=True), axis=1, keepdims=True)
            at = chunk * count + item
            out[at : at + 1, :] = jnp.broadcast_to(total, (1, out.shape[1]))


def score_products(even, odd, grads):
    return pl.pallas_call(
        score_kernel,
        in_specs=[in_vmem] * (2 + len(grads)),
        out_specs=in_vmem,
        out_shape=jax.ShapeDtypeStruct((len(grads) * grads[0].shape[1], 128), f32),
        compiler_params=params(),
        cost_estimate=cheap(),
        name="score_products",
    )(even, odd, *grads)


def output_kernel(*refs):
    found, out = refs[:-1], refs[-1]
    parts, groups, own_rows, jump = out.shape
    _, group, _, part = position(groups, parts)
    for pair in range(groups // 2):
        for odd in range(2):
            for away in range(parts):
                value = decode(found[pair][odd, away], jump)
                row = jnp.bitwise_xor(group, 2 * pair + odd)
                out[jnp.bitwise_xor(part, away), row] = value[:own_rows]


def output_rows(found, groups, parts, own_rows, jump):
    return pl.pallas_call(
        output_kernel,
        in_specs=[in_vmem] * len(found),
        out_specs=in_vmem,
        out_shape=jax.ShapeDtypeStruct((parts, groups, own_rows, jump), f32),
        compiler_params=params(),
        cost_estimate=cheap(),
        name="output_rows",
    )(*found)


def on_device(
    train_inputs,
    train_cotangents,
    query_inputs,
    query_cotangents,
    timesteps,
    input_basis,
    output_basis,
    eigenvalues,
):
    channels = output_basis.shape[0]
    shards = lax.axis_size("dp")
    factor = lax.axis_size("factor")
    groups, parts = shards // 2, factor // 2
    width = input_basis.shape[0] * shards
    depth = width // 4
    own_rows = channels // (groups * parts)
    high_rows = padded(own_rows, 8)
    jump = input_basis.shape[1]
    group, part = lax.axis_index("dp") % groups, lax.axis_index("factor") % parts
    early, late = 10**3, 10**10
    batch = train_inputs.shape[0]
    chunks = 2 if batch % 2 == 0 else 1
    rows = input_basis.shape[0]
    cut = padded(rows // 2, 16)

    def swap(array, away):
        return lax.ppermute(array, "dp", [(d, d ^ away) for d in range(shards)])

    def flip(array, away):
        return lax.ppermute(array, "factor", [(p, p ^ away) for p in range(factor)])

    def train(chunk, chosen):
        size = batch // chunks
        return train_gradients(
            chosen, train_inputs, train_cotangents, shards, parts, chunk * size, size, late if chunk else early
        )

    blocks = [((0, 0, 0, rows), input_basis)]
    for away in range(1, groups):
        if away != 3:
            blocks.append(((away, 0, 0, rows), swap(input_basis, away)))
    near = [((0, away, 0, rows), flip(input_basis, away)) for away in range(1, parts)]
    count = query_inputs.shape[0] * shards
    partial, chosen = query_partial(
        query_inputs, query_cotangents, output_basis, shards, groups, parts, own_rows, 1.0 / count
    )
    arrived = lax.all_to_all(partial, "dp", 0, 0)
    trained = [train(0, chosen)]
    blocks, near, trained, chosen, eigenvalues = fence_blocks(
        blocks, near, trained, chosen, eigenvalues
    )

    if groups > 3:
        blocks.append(((3, 0, 0, cut), swap(blocks[2][1][:cut], 1)))
        blocks.append(((3, 0, cut, rows), swap(blocks[1][1][cut:], 2)))
    trained += [train(chunk, chosen) for chunk in range(1, chunks)]
    eigen = []
    for away in range(parts):
        start = ((part ^ away) * groups + group) * own_rows
        lines = lax.dynamic_slice_in_dim(eigenvalues, start, own_rows, axis=0)
        if high_rows > own_rows:
            lines = jnp.pad(lines, ((0, high_rows - own_rows), (0, 0)), constant_values=1.0)
        eigen.append(flip(lines, away) if away else lines)
    blocks, near, trained, arrived, eigen = fence_blocks(blocks, near, trained, arrived, eigen)

    total, sent = merge(arrived, depth)
    other = flip(sent, parts)
    for away in range(1, parts):
        for (row, _, start, stop), piece in blocks[1:]:
            near.append(((row, away, start, stop), flip(piece, away)))
    blocks, near, total, other = fence_blocks(blocks, near, total, other)
    blocks = blocks + near

    own = project(total, other, blocks, groups, parts)
    other = swap(own, groups)
    own, other, eigen = fence((own, other, eigen))

    proj, keep, send = project_back(own, other, eigen, blocks, rows, groups, parts)
    other = flip(send, parts)
    mine = [proj[0]] + [flip(proj[away], away) for away in range(1, parts)]
    keep, other, mine = fence((keep, other, mine))

    power_keep = keep[:, depth : depth + 1].astype(f32)
    power_other = other[:, depth : depth + 1].astype(f32)
    power = jnp.maximum(power_keep, power_other) + 1.0
    values = keep.astype(f32) * jnp.exp2(power_keep - power)
    values += other.astype(f32) * jnp.exp2(power_other - power)
    marked = lax.broadcasted_iota(i32, keep.shape, 1) >= depth
    whole = jnp.where(marked, power, jnp.round(values)).astype(i16)
    even = [whole] + [swap(whole, away) for away in range(2, shards, 2)]
    mine = jnp.stack(mine)
    pair = [mine, swap(mine, 1)]
    even, pair = fence((even, pair))

    even, pair = jnp.stack(even), jnp.stack(pair)
    odd = swap(even, 1)
    found = [pair] + [swap(pair, away) for away in range(2, groups, 2)]
    even, odd, found = fence((even, odd, found))

    sums = score_products(even, odd, trained)
    terms = [sums[:, 0]]
    terms += [flip(terms[0], away) for away in range(1, factor)]
    while len(terms) > 1:
        terms = [terms[at] + terms[at + 1] for at in range(0, len(terms), 2)]
    raw_scores = terms[0]
    query_proj = output_rows(found, groups, parts, own_rows, jump).reshape(channels, jump)
    phase = (timesteps.astype(f32) / 1000.0 + 0.008) / 1.008 * (math.pi / 2)
    weight = jnp.sin(phase)
    scores = raw_scores * weight / math.sqrt(channels * width)
    return (scores, query_proj)


def solution(mesh):
    in_specs = (
        P("dp", None, None, None),
        P("dp", None, None, None),
        P("dp", None, None, None),
        P("dp", None, None, None),
        P("dp"),
        P("dp", "factor"),
        P(),
        P(None, "factor"),
    )
    out_specs = (P("dp"), P(None, "factor"))
    return jax.shard_map(
        on_device, mesh=mesh, in_specs=in_specs, out_specs=out_specs, check_vma=False
    )
```

```python
import functools
import math

import jax
import jax.numpy as jnp
from jax import lax
from jax.experimental import pallas as pl
from jax.experimental.pallas import tpu as pltpu
from jax.sharding import PartitionSpec as P

damping = 0.01
levels = 32000.0
bf16 = jnp.bfloat16
f32 = jnp.float32
i16 = jnp.int16
i32 = jnp.int32
first_dims = (((0,), (0,)), ((), ()))
last_dims = (((1,), (1,)), ((), ()))
fence = lax.optimization_barrier
mib = 2**20
in_vmem = pl.BlockSpec(memory_space=pltpu.VMEM)
anywhere = pl.BlockSpec(memory_space=pl.ANY)


def in_space(array, space):
    return pltpu.with_memory_space_constraint(array, space)


def in_hbm(array):
    return in_space(array, pltpu.HBM)


def padded(size, unit):
    return size + (-size) % unit


def with_scale(size):
    return size + 128 - size % 128


def cheap(flops=1000):
    return pl.CostEstimate(flops=flops, bytes_accessed=1000, transcendentals=0)


def params():
    return pltpu.CompilerParams(vmem_limit_bytes=24 * mib)


def position(groups, parts):
    me, place = lax.axis_index("dp"), lax.axis_index("factor")
    return me, lax.rem(me, groups), lax.div(place, parts), lax.rem(place, parts)


def power_of(*arrays):
    tops = [jnp.max(jnp.max(jnp.abs(a), axis=1, keepdims=True), axis=0, keepdims=True) for a in arrays]
    largest = functools.reduce(jnp.maximum, tops)
    return jnp.ceil(jnp.log(jnp.maximum(largest, 1e-30)) * (1 / math.log(2.0)))


def encode(array, power):
    return jnp.round(array * (jnp.exp2(-power) * levels)).astype(i32).astype(i16)


def put(ref, at, array, power):
    rows, size = array.shape
    wide = ref.shape[-1]
    marks = jnp.broadcast_to(power, (rows, wide - size)).astype(i32).astype(i16)
    if at is None:
        ref[:, :size] = encode(array, power)
        ref[:, size:] = marks
    else:
        ref[at, :, :size] = encode(array, power)
        ref[at, :, size:] = marks


def decode(sent, size):
    values = sent[:, :size].astype(i32).astype(f32)
    power = sent[:, size : size + 1].astype(i32).astype(f32)
    return values * (jnp.exp2(power) * (1 / levels))


def halves(array):
    upper = array.astype(bf16)
    lower = (array - upper.astype(f32)).astype(bf16)
    return upper, lower


def both_halves(array):
    upper = array.astype(bf16).astype(f32)
    return jnp.concatenate([upper, array - upper], axis=0).astype(bf16)


def shifted_inputs(activations):
    rows, cols, channels = activations.shape
    edge = jnp.zeros((rows, 1, channels), activations.dtype)
    before = jnp.concatenate([edge, activations[:, :-1]], axis=1)
    after = jnp.concatenate([activations[:, 1:], edge], axis=1)
    blank = jnp.zeros((cols, channels), activations.dtype)
    return [
        jnp.concatenate([blank, part.reshape(rows * cols, channels), blank], axis=0)
        for part in (before, activations, after)
    ]


def patch_columns(shifted, rows, cols, start, stop):
    channels = shifted[0].shape[1]
    taps = []
    for tap in range(start // channels, -(-stop // channels)):
        row_off, col_off = divmod(tap, 3)
        low, high = max(start - tap * channels, 0), min(stop - tap * channels, channels)
        taps.append(shifted[col_off][row_off * cols : (row_off + rows) * cols, low:high])
    return jnp.concatenate(taps, axis=1)


def fence_blocks(blocks, near, *others):
    held, rest, others = fence(([b for _, b in blocks], [b for _, b in near], others))
    named = [(spot, b) for (spot, _), b in zip(blocks, held)]
    return named, [(spot, b) for (spot, _), b in zip(near, rest)], *others


def query_kernel(x_ref, c_ref, basis_ref, out, chosen_ref, total, *, groups, parts, own_rows, scale):
    queries, rows, cols, channels = x_ref.shape
    shards, high_rows, depth = total.shape
    _, _, side, part = position(groups, parts)
    span = groups * high_rows
    row_at = lax.broadcasted_iota(i32, (channels, span), 0)
    col_at = lax.broadcasted_iota(i32, (channels, span), 1)
    group, item = lax.div(col_at, high_rows), lax.rem(col_at, high_rows)
    wanted = part * groups * own_rows + group * own_rows + item
    chosen = jnp.where((row_at == wanted) & (item < own_rows), 1.0, 0.0).astype(bf16)
    own_basis = jnp.dot(basis_ref[...], chosen, preferred_element_type=f32).astype(bf16)
    chosen_ref[...] = own_basis

    for value in range(2):

        @pl.when(side == value)
        def _(value=value):
            sums = [jnp.zeros((span, depth), f32) for _ in range(2)]
            for query in range(queries):
                cot = c_ref[query].reshape(rows * cols, channels)
                upper, lower = halves(jnp.dot(cot, own_basis, preferred_element_type=f32))
                shifted = shifted_inputs(x_ref[query])
                for half in range(2):
                    start = (2 * half + value) * depth
                    patches = patch_columns(shifted, rows, cols, start, start + depth)
                    for piece in (upper, lower):
                        sums[half] += lax.dot_general(
                            piece, patches, first_dims, preferred_element_type=f32
                        )
            for half in range(2):
                for group in range(groups):
                    total[half * groups + group] = (
                        sums[half][group * high_rows : (group + 1) * high_rows] * scale
                    )

    power = power_of(*[total[shard] for shard in range(shards)])
    for shard in range(shards):
        put(out, shard, total[shard], power)


def query_partial(x, cot, basis, shards, groups, parts, own_rows, scale):
    channels = x.shape[-1]
    high_rows = padded(own_rows, 8)
    depth = 9 * channels // 4
    return pl.pallas_call(
        functools.partial(
            query_kernel, groups=groups, parts=parts, own_rows=own_rows, scale=scale
        ),
        in_specs=[in_vmem] * 3,
        out_specs=[in_vmem] * 2,
        out_shape=[
            jax.ShapeDtypeStruct((shards, high_rows, with_scale(depth)), i16),
            jax.ShapeDtypeStruct((channels, groups * high_rows), bf16),
        ],
        scratch_shapes=[pltpu.VMEM((shards, high_rows, depth), f32)],
        compiler_params=params(),
        cost_estimate=cheap(),
        name="query_gradient",
    )(in_hbm(x), in_hbm(cot), in_hbm(basis))


def train_kernel(basis_ref, x_ref, c_ref, out_ref, *, parts):
    _, rows, cols, channels = x_ref.shape
    shards, _, high_rows, depth = out_ref.shape
    groups = shards // 2
    _, _, side, _ = position(groups, parts)
    cot = c_ref[0].reshape(rows * cols, channels)
    rotated = jnp.dot(cot, basis_ref[...], preferred_element_type=f32).astype(bf16)
    for value in range(2):

        @pl.when(side == value)
        def _(value=value):
            shifted = shifted_inputs(x_ref[0])
            for half in range(2):
                start = (2 * half + value) * depth
                patches = patch_columns(shifted, rows, cols, start, start + depth)
                grad = lax.dot_general(rotated, patches, first_dims, preferred_element_type=f32)
                for group in range(groups):
                    out_ref[half * groups + group, 0] = grad[
                        group * high_rows : (group + 1) * high_rows
                    ]


def train_gradients(chosen, x, cot, shards, parts, first, count, flops):
    _, rows, cols, channels = x.shape
    high_rows = chosen.shape[1] // (shards // 2)
    depth = 9 * channels // 4
    spec = pl.BlockSpec((1, rows, cols, channels), lambda i: (first + i, 0, 0, 0))
    return pl.pallas_call(
        functools.partial(train_kernel, parts=parts),
        grid=(count,),
        in_specs=[pl.BlockSpec(chosen.shape, lambda i: (0, 0)), spec, spec],
        out_specs=pl.BlockSpec((shards, 1, high_rows, depth), lambda i: (0, i, 0, 0)),
        out_shape=pltpu.HBM((shards, count, high_rows, depth), f32),
        compiler_params=params(),
        cost_estimate=cheap(flops),
        name="train_gradients",
    )(chosen, in_hbm(x), in_hbm(cot))


def merge_kernel(arrived, keep_ref, send_ref):
    total = decode(arrived[0], keep_ref.shape[1])
    for shard in range(1, arrived.shape[0]):
        total += decode(arrived[shard], keep_ref.shape[1])
    keep_ref[...] = total
    put(send_ref, None, total, power_of(total))


def merge(arrived, depth):
    _, high_rows, wide = arrived.shape
    return pl.pallas_call(
        merge_kernel,
        in_specs=[in_vmem],
        out_specs=[in_vmem] * 2,
        out_shape=[
            jax.ShapeDtypeStruct((high_rows, depth), f32),
            jax.ShapeDtypeStruct((high_rows, wide), i16),
        ],
        compiler_params=params(),
        cost_estimate=cheap(),
        name="merge",
    )(arrived)


def project_kernel(own_ref, other_ref, *refs, spots, groups, parts):
    pieces, (out, stacked) = refs[: len(spots)], refs[len(spots) :]
    high_rows, depth = own_ref.shape
    rows = depth * 2 // groups
    _, group, side, _ = position(groups, parts)
    own, other = own_ref[...], decode(other_ref, depth)
    for half, value in enumerate(
        (jnp.where(side == 0, own, other), jnp.where(side == 0, other, own))
    ):
        both = both_halves(value)
        for at in range(groups // 2):
            stacked[half * (groups // 2) + at] = both[:, at * rows : (at + 1) * rows]
    results = [0.0] * parts
    for piece, (row, part, start, stop) in zip(pieces, spots):
        left = stacked[jnp.bitwise_xor(group, row)][:, start:stop]
        results[part] += jnp.dot(left, piece[...], preferred_element_type=f32)
    results = [total[:high_rows] + total[high_rows:] for total in results]
    power = power_of(*results)
    for part in range(parts):
        put(out, part, results[part], power)


def project(own, other, blocks, groups, parts):
    spots = [spot for spot, _ in blocks]
    pieces = [piece for _, piece in blocks]
    high_rows, depth = own.shape
    return pl.pallas_call(
        functools.partial(project_kernel, spots=spots, groups=groups, parts=parts),
        in_specs=[in_vmem] * (2 + len(pieces)),
        out_specs=in_vmem,
        out_shape=jax.ShapeDtypeStruct((parts, high_rows, with_scale(pieces[0].shape[1])), i16),
        scratch_shapes=[pltpu.VMEM((groups, 2 * high_rows, depth * 2 // groups), bf16)],
        compiler_params=params(),
        cost_estimate=cheap(),
        name="project",
    )(own, other, *pieces)


def back_kernel(own_ref, other_ref, *refs, spots, groups, parts):
    eigen, refs = refs[:parts], refs[parts:]
    pieces, refs = refs[: len(spots)], refs[len(spots) :]
    proj_ref, keep_ref, send_ref, ordered = refs
    high_rows, width = eigen[0].shape
    _, group, side, _ = position(groups, parts)
    results, stacked = [], []
    for part in range(parts):
        total = decode(own_ref[part], width) + decode(other_ref[part], width)
        results.append(total / (eigen[part][...] + damping))
        stacked.append(both_halves(results[part]))
    sums = {}
    for piece, (row, part, start, stop) in zip(pieces, spots):
        total = lax.dot_general(
            stacked[part], piece[...], last_dims, preferred_element_type=f32
        )
        sums[row, start, stop] = sums.get((row, start, stop), 0.0) + total
    for (row, start, stop), total in sums.items():
        ordered[jnp.bitwise_xor(group, row), :, start:stop] = total[:high_rows] + total[high_rows:]
    sides = [
        jnp.concatenate(
            [ordered[half * (groups // 2) + at] for at in range(groups // 2)], axis=1
        )
        for half in range(2)
    ]
    keep = jnp.where(side == 0, sides[0], sides[1])
    send = jnp.where(side == 0, sides[1], sides[0])
    power = power_of(keep, send)
    put(keep_ref, None, keep, power)
    put(send_ref, None, send, power)
    power = power_of(*results)
    for part in range(parts):
        put(proj_ref, part, results[part], power)


def project_back(own, other, eigen, blocks, rows, groups, parts):
    spots = [spot for spot, _ in blocks]
    pieces = [piece for _, piece in blocks]
    high_rows = eigen[0].shape[0]
    half = jax.ShapeDtypeStruct((high_rows, with_scale(groups * rows // 2)), i16)
    return pl.pallas_call(
        functools.partial(back_kernel, spots=spots, groups=groups, parts=parts),
        in_specs=[in_vmem] * (2 + parts + len(pieces)),
        out_specs=[in_vmem] * 3,
        out_shape=[jax.ShapeDtypeStruct(own.shape, i16), half, half],
        scratch_shapes=[pltpu.VMEM((groups, high_rows, rows), f32)],
        compiler_params=params(),
        cost_estimate=cheap(),
        name="project_back",
    )(own, other, *eigen, *pieces)


def score_kernel(found, *refs, offset):
    grads, out = refs[:-1], refs[-1]
    high_rows, depth = grads[0].shape[2:]
    me = lax.axis_index("dp")
    blocks = []
    for pair in range(found.shape[0]):
        at = jnp.bitwise_xor(me, 2 * pair + offset)
        blocks.append((at, decode(found[pair], depth)))
    line = 0
    for grad in grads:
        for item in range(grad.shape[1]):
            total = jnp.zeros((high_rows, depth), f32)
            for at, values in blocks:
                total += grad[at, item] * values
            total = jnp.sum(jnp.sum(total, axis=0, keepdims=True), axis=1, keepdims=True)
            out[line : line + 1, :] = jnp.broadcast_to(total, (1, out.shape[1]))
            line += 1


def score_products(found, grads, offset, flops):
    return pl.pallas_call(
        functools.partial(score_kernel, offset=offset),
        in_specs=[in_vmem] * (1 + len(grads)),
        out_specs=in_vmem,
        out_shape=jax.ShapeDtypeStruct((sum(grad.shape[1] for grad in grads), 128), f32),
        compiler_params=params(),
        cost_estimate=cheap(flops),
        name="score_products",
    )(found, *grads)


def output_kernel(own_ref, *refs):
    found, out = (own_ref,) + refs[:-1], refs[-1]
    parts, groups, own_rows, jump = out.shape
    _, group, _, part = position(groups, parts)
    for away in range(parts):
        for row in range(groups):
            value = decode(found[away][row], jump)
            out[jnp.bitwise_xor(part, away), jnp.bitwise_xor(group, row)] = value[:own_rows]


def output_rows(found, groups, parts, own_rows, jump):
    return pl.pallas_call(
        output_kernel,
        in_specs=[in_vmem] * len(found),
        out_specs=in_vmem,
        out_shape=jax.ShapeDtypeStruct((parts, groups, own_rows, jump), f32),
        compiler_params=params(),
        cost_estimate=cheap(),
        name="output_rows",
    )(*found)


def on_device(
    train_inputs,
    train_cotangents,
    query_inputs,
    query_cotangents,
    timesteps,
    input_basis,
    output_basis,
    eigenvalues,
):
    channels = output_basis.shape[0]
    shards = lax.axis_size("dp")
    factor = lax.axis_size("factor")
    groups, parts = shards // 2, factor // 2
    width = input_basis.shape[0] * shards
    depth = width // 4
    own_rows = channels // (groups * parts)
    high_rows = padded(own_rows, 8)
    jump = input_basis.shape[1]
    group, part = lax.axis_index("dp") % groups, lax.axis_index("factor") % parts
    batch = train_inputs.shape[0]
    bounds = [0, batch * 4 // 8, batch * 8 // 8, batch]
    rows = input_basis.shape[0]
    cut = padded(rows // 2, 16)

    def swap(array, away):
        return lax.ppermute(array, "dp", [(d, d ^ away) for d in range(shards)])

    def flip(array, away):
        return lax.ppermute(array, "factor", [(p, p ^ away) for p in range(factor)])

    def train(chunk, chosen, flops=10**3):
        first, last = bounds[chunk], bounds[chunk + 1]
        if first == last:
            return []
        inputs = (train_inputs, train_cotangents)
        return [
            train_gradients(chosen, *inputs, shards, parts, first, last - first, flops)
        ]

    blocks = [((0, 0, 0, rows), input_basis)]
    for away in range(1, groups):
        if away != 3:
            blocks.append(((away, 0, 0, rows), swap(input_basis, away)))
    near = [((0, away, 0, rows), flip(input_basis, away)) for away in range(1, parts)]
    count = query_inputs.shape[0] * shards
    partial, chosen = query_partial(
        query_inputs, query_cotangents, output_basis, shards, groups, parts, own_rows, 1.0 / count
    )
    arrived = lax.all_to_all(partial, "dp", 0, 0)
    trained = train(0, chosen)
    blocks, near, trained, chosen, eigenvalues = fence_blocks(
        blocks, near, trained, chosen, eigenvalues
    )

    if groups > 3:
        blocks.append(((3, 0, 0, cut), swap(blocks[2][1][:cut], 1)))
        blocks.append(((3, 0, cut, rows), swap(blocks[1][1][cut:], 2)))
    trained += train(1, chosen, 10**10)
    eigen = []
    for away in range(parts):
        start = ((part ^ away) * groups + group) * own_rows
        lines = lax.dynamic_slice_in_dim(eigenvalues, start, own_rows, axis=0)
        if high_rows > own_rows:
            lines = jnp.pad(lines, ((0, high_rows - own_rows), (0, 0)), constant_values=1.0)
        eigen.append(flip(lines, away) if away else lines)
    blocks, near, trained, chosen, arrived, eigen = fence_blocks(
        blocks, near, trained, chosen, arrived, eigen
    )

    total, sent = merge(arrived, depth)
    other = flip(sent, parts)
    for away in range(1, parts):
        for (row, _, start, stop), piece in blocks[1:]:
            near.append(((row, away, start, stop), flip(piece, away)))
    trained += train(2, chosen)
    blocks, near, total, other, trained = fence_blocks(blocks, near, total, other, trained)
    blocks = blocks + near

    own = project(total, other, blocks, groups, parts)
    other = swap(own, groups)
    own, other, eigen = fence((own, other, eigen))

    proj, keep, send = project_back(own, other, eigen, blocks, rows, groups, parts)
    other = flip(send, parts)
    pair = [proj, swap(proj, 1)]
    keep, other = fence((keep, other))

    power_keep = keep[:, depth : depth + 1].astype(f32)
    power_other = other[:, depth : depth + 1].astype(f32)
    power = jnp.maximum(power_keep, power_other) + 1.0
    values = keep.astype(f32) * jnp.exp2(power_keep - power)
    values += other.astype(f32) * jnp.exp2(power_other - power)
    marked = lax.broadcasted_iota(i32, keep.shape, 1) >= depth
    whole = jnp.where(marked, power, jnp.round(values)).astype(i16)
    even = [whole] + [swap(whole, away) for away in range(2, shards, 2)]
    even, pair, timesteps = fence((even, pair, timesteps))

    even, pair = jnp.stack(even), jnp.stack(pair)
    odd = swap(even, 1)
    found = [pair] + [swap(pair, away) for away in range(2, groups, 2)]
    phase = (timesteps.astype(f32) / 1000.0 + 0.008) / 1.008 * (math.pi / 2)
    weight = jnp.sin(phase) * (1 / math.sqrt(channels * width))
    sums = score_products(even, trained, 0, 10**10)
    odd, found, sums, weight = fence((odd, found, sums, weight))

    sums = sums + score_products(odd, trained, 1, 10**3)
    found = jnp.concatenate(found)
    terms = [sums[:, 0]]
    terms += [flip(terms[0], away) for away in range(1, factor)]
    rows_found = [found[:, 0]] + [flip(found[:, away], away) for away in range(1, parts)]
    query_proj = output_rows(rows_found, groups, parts, own_rows, jump).reshape(channels, jump)
    terms, query_proj = fence((terms, query_proj))
    while len(terms) > 1:
        terms = [terms[at] + terms[at + 1] for at in range(0, len(terms), 2)]
    return (terms[0] * weight, query_proj)


def solution(mesh):
    in_specs = (
        P("dp", None, None, None),
        P("dp", None, None, None),
        P("dp", None, None, None),
        P("dp", None, None, None),
        P("dp"),
        P("dp", "factor"),
        P(),
        P(None, "factor"),
    )
    out_specs = (P("dp"), P(None, "factor"))
    return jax.shard_map(
        on_device, mesh=mesh, in_specs=in_specs, out_specs=out_specs, check_vma=False
    )
```

```python
import functools
import math

import jax
import jax.numpy as jnp
from jax import lax
from jax.experimental import pallas as pl
from jax.experimental.pallas import tpu as pltpu
from jax.sharding import PartitionSpec as P

damping = 0.01
levels = 32000.0
bf16 = jnp.bfloat16
f32 = jnp.float32
i16 = jnp.int16
i32 = jnp.int32
first_dims = (((0,), (0,)), ((), ()))
last_dims = (((1,), (1,)), ((), ()))
fence = lax.optimization_barrier
mib = 2**20
in_vmem = pl.BlockSpec(memory_space=pltpu.VMEM)
anywhere = pl.BlockSpec(memory_space=pl.ANY)


def in_space(array, space):
    return pltpu.with_memory_space_constraint(array, space)


def in_hbm(array):
    return in_space(array, pltpu.HBM)


def padded(size, unit):
    return size + (-size) % unit


def with_scale(size):
    return size + 128 - size % 128


def cheap(flops=1000):
    return pl.CostEstimate(flops=flops, bytes_accessed=1000, transcendentals=0)


def params():
    return pltpu.CompilerParams(vmem_limit_bytes=24 * mib)


def position(groups, parts):
    me, place = lax.axis_index("dp"), lax.axis_index("factor")
    return me, lax.rem(me, groups), lax.div(place, parts), lax.rem(place, parts)


def power_of(*arrays):
    tops = [jnp.max(jnp.max(jnp.abs(a), axis=1, keepdims=True), axis=0, keepdims=True) for a in arrays]
    largest = functools.reduce(jnp.maximum, tops)
    return jnp.ceil(jnp.log(jnp.maximum(largest, 1e-30)) * (1 / math.log(2.0)))


def encode(array, power):
    return jnp.round(array * (jnp.exp2(-power) * levels)).astype(i32).astype(i16)


def put(ref, at, array, power):
    rows, size = array.shape
    wide = ref.shape[-1]
    marks = jnp.broadcast_to(power, (rows, wide - size)).astype(i32).astype(i16)
    if at is None:
        ref[:, :size] = encode(array, power)
        ref[:, size:] = marks
    else:
        ref[at, :, :size] = encode(array, power)
        ref[at, :, size:] = marks


def decode(sent, size):
    values = sent[:, :size].astype(i32).astype(f32)
    power = sent[:, size : size + 1].astype(i32).astype(f32)
    return values * (jnp.exp2(power) * (1 / levels))


def halves(array):
    upper = array.astype(bf16)
    lower = (array - upper.astype(f32)).astype(bf16)
    return upper, lower


def both_halves(array):
    upper = array.astype(bf16).astype(f32)
    return jnp.concatenate([upper, array - upper], axis=0).astype(bf16)


def shifted_inputs(activations):
    rows, cols, channels = activations.shape
    edge = jnp.zeros((rows, 1, channels), activations.dtype)
    before = jnp.concatenate([edge, activations[:, :-1]], axis=1)
    after = jnp.concatenate([activations[:, 1:], edge], axis=1)
    blank = jnp.zeros((cols, channels), activations.dtype)
    return [
        jnp.concatenate([blank, part.reshape(rows * cols, channels), blank], axis=0)
        for part in (before, activations, after)
    ]


def patch_columns(shifted, rows, cols, start, stop):
    channels = shifted[0].shape[1]
    taps = []
    for tap in range(start // channels, -(-stop // channels)):
        row_off, col_off = divmod(tap, 3)
        low, high = max(start - tap * channels, 0), min(stop - tap * channels, channels)
        taps.append(shifted[col_off][row_off * cols : (row_off + rows) * cols, low:high])
    return jnp.concatenate(taps, axis=1)


def fence_blocks(blocks, near, *others):
    held, rest, others = fence(([b for _, b in blocks], [b for _, b in near], others))
    named = [(spot, b) for (spot, _), b in zip(blocks, held)]
    return named, [(spot, b) for (spot, _), b in zip(near, rest)], *others


def query_kernel(x_ref, c_ref, basis_ref, out, chosen_ref, total, *, groups, parts, own_rows, scale):
    queries, rows, cols, channels = x_ref.shape
    shards, high_rows, depth = total.shape
    _, _, side, part = position(groups, parts)
    span = groups * high_rows
    row_at = lax.broadcasted_iota(i32, (channels, span), 0)
    col_at = lax.broadcasted_iota(i32, (channels, span), 1)
    group, item = lax.div(col_at, high_rows), lax.rem(col_at, high_rows)
    wanted = part * groups * own_rows + group * own_rows + item
    chosen = jnp.where((row_at == wanted) & (item < own_rows), 1.0, 0.0).astype(bf16)
    own_basis = jnp.dot(basis_ref[...], chosen, preferred_element_type=f32).astype(bf16)
    chosen_ref[...] = own_basis

    for value in range(2):

        @pl.when(side == value)
        def _(value=value):
            sums = [jnp.zeros((span, depth), f32) for _ in range(2)]
            for query in range(queries):
                cot = c_ref[query].reshape(rows * cols, channels)
                upper, lower = halves(jnp.dot(cot, own_basis, preferred_element_type=f32))
                shifted = shifted_inputs(x_ref[query])
                for half in range(2):
                    start = (2 * half + value) * depth
                    patches = patch_columns(shifted, rows, cols, start, start + depth)
                    for piece in (upper, lower):
                        sums[half] += lax.dot_general(
                            piece, patches, first_dims, preferred_element_type=f32
                        )
            for half in range(2):
                for group in range(groups):
                    total[half * groups + group] = (
                        sums[half][group * high_rows : (group + 1) * high_rows] * scale
                    )

    power = power_of(*[total[shard] for shard in range(shards)])
    for shard in range(shards):
        put(out, shard, total[shard], power)


def query_partial(x, cot, basis, shards, groups, parts, own_rows, scale):
    channels = x.shape[-1]
    high_rows = padded(own_rows, 8)
    depth = 9 * channels // 4
    return pl.pallas_call(
        functools.partial(
            query_kernel, groups=groups, parts=parts, own_rows=own_rows, scale=scale
        ),
        in_specs=[in_vmem] * 3,
        out_specs=[in_vmem] * 2,
        out_shape=[
            jax.ShapeDtypeStruct((shards, high_rows, with_scale(depth)), i16),
            jax.ShapeDtypeStruct((channels, groups * high_rows), bf16),
        ],
        scratch_shapes=[pltpu.VMEM((shards, high_rows, depth), f32)],
        compiler_params=params(),
        cost_estimate=cheap(),
        name="query_gradient",
    )(in_hbm(x), in_hbm(cot), in_hbm(basis))


def train_kernel(basis_ref, x_ref, c_ref, out_ref, *, parts):
    _, rows, cols, channels = x_ref.shape
    shards, _, high_rows, depth = out_ref.shape
    groups = shards // 2
    _, _, side, _ = position(groups, parts)
    cot = c_ref[0].reshape(rows * cols, channels)
    rotated = jnp.dot(cot, basis_ref[...], preferred_element_type=f32).astype(bf16)
    for value in range(2):

        @pl.when(side == value)
        def _(value=value):
            shifted = shifted_inputs(x_ref[0])
            for half in range(2):
                start = (2 * half + value) * depth
                patches = patch_columns(shifted, rows, cols, start, start + depth)
                grad = lax.dot_general(rotated, patches, first_dims, preferred_element_type=f32)
                for group in range(groups):
                    out_ref[half * groups + group, 0] = grad[
                        group * high_rows : (group + 1) * high_rows
                    ]


def train_gradients(chosen, x, cot, shards, parts, first, count, flops):
    _, rows, cols, channels = x.shape
    high_rows = chosen.shape[1] // (shards // 2)
    depth = 9 * channels // 4
    spec = pl.BlockSpec((1, rows, cols, channels), lambda i: (first + i, 0, 0, 0))
    return pl.pallas_call(
        functools.partial(train_kernel, parts=parts),
        grid=(count,),
        in_specs=[pl.BlockSpec(chosen.shape, lambda i: (0, 0)), spec, spec],
        out_specs=pl.BlockSpec((shards, 1, high_rows, depth), lambda i: (0, i, 0, 0)),
        out_shape=pltpu.HBM((shards, count, high_rows, depth), f32),
        compiler_params=params(),
        cost_estimate=cheap(flops),
        name="train_gradients",
    )(chosen, in_hbm(x), in_hbm(cot))


def merge_kernel(arrived, keep_ref, send_ref):
    total = decode(arrived[0], keep_ref.shape[1])
    for shard in range(1, arrived.shape[0]):
        total += decode(arrived[shard], keep_ref.shape[1])
    keep_ref[...] = total
    put(send_ref, None, total, power_of(total))


def merge(arrived, depth):
    _, high_rows, wide = arrived.shape
    return pl.pallas_call(
        merge_kernel,
        in_specs=[in_vmem],
        out_specs=[in_vmem] * 2,
        out_shape=[
            jax.ShapeDtypeStruct((high_rows, depth), f32),
            jax.ShapeDtypeStruct((high_rows, wide), i16),
        ],
        compiler_params=params(),
        cost_estimate=cheap(),
        name="merge",
    )(arrived)


def project_kernel(own_ref, other_ref, *refs, spots, groups, parts):
    pieces, (out, stacked) = refs[: len(spots)], refs[len(spots) :]
    high_rows, depth = own_ref.shape
    rows = depth * 2 // groups
    _, group, side, _ = position(groups, parts)
    own, other = own_ref[...], decode(other_ref, depth)
    for half, value in enumerate(
        (jnp.where(side == 0, own, other), jnp.where(side == 0, other, own))
    ):
        both = both_halves(value)
        for at in range(groups // 2):
            stacked[half * (groups // 2) + at] = both[:, at * rows : (at + 1) * rows]
    results = [0.0] * parts
    for piece, (row, part, start, stop) in zip(pieces, spots):
        left = stacked[jnp.bitwise_xor(group, row)][:, start:stop]
        results[part] += jnp.dot(left, piece[...], preferred_element_type=f32)
    results = [total[:high_rows] + total[high_rows:] for total in results]
    power = power_of(*results)
    for part in range(parts):
        put(out, part, results[part], power)


def project(own, other, blocks, groups, parts):
    spots = [spot for spot, _ in blocks]
    pieces = [piece for _, piece in blocks]
    high_rows, depth = own.shape
    return pl.pallas_call(
        functools.partial(project_kernel, spots=spots, groups=groups, parts=parts),
        in_specs=[in_vmem] * (2 + len(pieces)),
        out_specs=in_vmem,
        out_shape=jax.ShapeDtypeStruct((parts, high_rows, with_scale(pieces[0].shape[1])), i16),
        scratch_shapes=[pltpu.VMEM((groups, 2 * high_rows, depth * 2 // groups), bf16)],
        compiler_params=params(),
        cost_estimate=cheap(),
        name="project",
    )(own, other, *pieces)


def back_kernel(own_ref, other_ref, *refs, spots, groups, parts):
    eigen, refs = refs[:parts], refs[parts:]
    pieces, refs = refs[: len(spots)], refs[len(spots) :]
    proj_ref, keep_ref, send_ref, ordered = refs
    high_rows, width = eigen[0].shape
    _, group, side, _ = position(groups, parts)
    results, stacked = [], []
    for part in range(parts):
        total = decode(own_ref[part], width) + decode(other_ref[part], width)
        results.append(total / (eigen[part][...] + damping))
        stacked.append(both_halves(results[part]))
    sums = {}
    for piece, (row, part, start, stop) in zip(pieces, spots):
        total = lax.dot_general(
            stacked[part], piece[...], last_dims, preferred_element_type=f32
        )
        sums[row, start, stop] = sums.get((row, start, stop), 0.0) + total
    for (row, start, stop), total in sums.items():
        ordered[jnp.bitwise_xor(group, row), :, start:stop] = total[:high_rows] + total[high_rows:]
    sides = [
        jnp.concatenate(
            [ordered[half * (groups // 2) + at] for at in range(groups // 2)], axis=1
        )
        for half in range(2)
    ]
    keep = jnp.where(side == 0, sides[0], sides[1])
    send = jnp.where(side == 0, sides[1], sides[0])
    power = power_of(keep, send)
    put(keep_ref, None, keep, power)
    put(send_ref, None, send, power)
    power = power_of(*results)
    for part in range(parts):
        put(proj_ref, part, results[part], power)


def project_back(own, other, eigen, blocks, rows, groups, parts):
    spots = [spot for spot, _ in blocks]
    pieces = [piece for _, piece in blocks]
    high_rows = eigen[0].shape[0]
    half = jax.ShapeDtypeStruct((high_rows, with_scale(groups * rows // 2)), i16)
    return pl.pallas_call(
        functools.partial(back_kernel, spots=spots, groups=groups, parts=parts),
        in_specs=[in_vmem] * (2 + parts + len(pieces)),
        out_specs=[in_vmem] * 3,
        out_shape=[jax.ShapeDtypeStruct(own.shape, i16), half, half],
        scratch_shapes=[pltpu.VMEM((groups, high_rows, rows), f32)],
        compiler_params=params(),
        cost_estimate=cheap(),
        name="project_back",
    )(own, other, *eigen, *pieces)


def score_kernel(found, *refs, offset):
    grads, out = refs[:-1], refs[-1]
    high_rows, depth = grads[0].shape[2:]
    me = lax.axis_index("dp")
    blocks = []
    for pair in range(found.shape[0]):
        at = jnp.bitwise_xor(me, 2 * pair + offset)
        blocks.append((at, decode(found[pair], depth)))
    line = 0
    for grad in grads:
        for item in range(grad.shape[1]):
            total = jnp.zeros((high_rows, depth), f32)
            for at, values in blocks:
                total += grad[at, item] * values
            total = jnp.sum(jnp.sum(total, axis=0, keepdims=True), axis=1, keepdims=True)
            out[line : line + 1, :] = jnp.broadcast_to(total, (1, out.shape[1]))
            line += 1


def score_products(found, grads, offset, flops):
    return pl.pallas_call(
        functools.partial(score_kernel, offset=offset),
        in_specs=[in_vmem] * (1 + len(grads)),
        out_specs=in_vmem,
        out_shape=jax.ShapeDtypeStruct((sum(grad.shape[1] for grad in grads), 128), f32),
        compiler_params=params(),
        cost_estimate=cheap(flops),
        name="score_products",
    )(found, *grads)


def output_kernel(own_ref, *refs):
    found, out = (own_ref,) + refs[:-1], refs[-1]
    parts, groups, own_rows, jump = out.shape
    _, group, _, part = position(groups, parts)
    for away in range(parts):
        for row in range(groups):
            value = decode(found[away][row], jump)
            out[jnp.bitwise_xor(part, away), jnp.bitwise_xor(group, row)] = value[:own_rows]


def output_rows(found, groups, parts, own_rows, jump):
    return pl.pallas_call(
        output_kernel,
        in_specs=[in_vmem] * len(found),
        out_specs=in_vmem,
        out_shape=jax.ShapeDtypeStruct((parts, groups, own_rows, jump), f32),
        compiler_params=params(),
        cost_estimate=cheap(),
        name="output_rows",
    )(*found)


def on_device(
    train_inputs,
    train_cotangents,
    query_inputs,
    query_cotangents,
    timesteps,
    input_basis,
    output_basis,
    eigenvalues,
):
    channels = output_basis.shape[0]
    shards = lax.axis_size("dp")
    factor = lax.axis_size("factor")
    groups, parts = shards // 2, factor // 2
    width = input_basis.shape[0] * shards
    depth = width // 4
    own_rows = channels // (groups * parts)
    high_rows = padded(own_rows, 8)
    jump = input_basis.shape[1]
    group, part = lax.axis_index("dp") % groups, lax.axis_index("factor") % parts
    batch = train_inputs.shape[0]
    bounds = [0, batch * 4 // 8, batch * 8 // 8, batch]
    rows = input_basis.shape[0]
    cut = padded(rows // 2, 16)

    def swap(array, away):
        return lax.ppermute(array, "dp", [(d, d ^ away) for d in range(shards)])

    def flip(array, away):
        return lax.ppermute(array, "factor", [(p, p ^ away) for p in range(factor)])

    def train(chunk, chosen, flops=10**3):
        first, last = bounds[chunk], bounds[chunk + 1]
        if first == last:
            return []
        inputs = (train_inputs, train_cotangents)
        return [
            train_gradients(chosen, *inputs, shards, parts, first, last - first, flops)
        ]

    blocks = [((0, 0, 0, rows), input_basis)]
    for away in range(1, groups):
        if away != 3:
            blocks.append(((away, 0, 0, rows), swap(input_basis, away)))
    near = [((0, away, 0, rows), flip(input_basis, away)) for away in range(1, parts)]
    count = query_inputs.shape[0] * shards
    partial, chosen = query_partial(
        query_inputs, query_cotangents, output_basis, shards, groups, parts, own_rows, 1.0 / count
    )
    arrived = lax.all_to_all(partial, "dp", 0, 0)
    trained = train(0, chosen)
    eigen = []
    for away in range(parts):
        start = ((part ^ away) * groups + group) * own_rows
        lines = lax.dynamic_slice_in_dim(eigenvalues, start, own_rows, axis=0)
        if high_rows > own_rows:
            lines = jnp.pad(lines, ((0, high_rows - own_rows), (0, 0)), constant_values=1.0)
        eigen.append(lines)
    blocks, near, trained, chosen, eigen = fence_blocks(blocks, near, trained, chosen, eigen)

    if groups > 3:
        blocks.append(((3, 0, 0, cut), swap(blocks[2][1][:cut], 1)))
        blocks.append(((3, 0, cut, rows), swap(blocks[1][1][cut:], 2)))
    trained += train(1, chosen, 10**10)
    eigen = [flip(lines, away) if away else lines for away, lines in enumerate(eigen)]
    blocks, near, trained, chosen, arrived, eigen = fence_blocks(
        blocks, near, trained, chosen, arrived, eigen
    )

    total, sent = merge(arrived, depth)
    other = flip(sent, parts)
    for away in range(1, parts):
        for (row, _, start, stop), piece in blocks[1:]:
            near.append(((row, away, start, stop), flip(piece, away)))
    trained += train(2, chosen)
    blocks, near, total, other, trained = fence_blocks(blocks, near, total, other, trained)
    blocks = blocks + near

    own = project(total, other, blocks, groups, parts)
    other = swap(own, groups)
    own, other, eigen = fence((own, other, eigen))

    proj, keep, send = project_back(own, other, eigen, blocks, rows, groups, parts)
    other = flip(send, parts)
    pair = [proj, swap(proj, 1)]
    keep, other = fence((keep, other))

    power_keep = keep[:, depth : depth + 1].astype(f32)
    power_other = other[:, depth : depth + 1].astype(f32)
    power = jnp.maximum(power_keep, power_other) + 1.0
    values = keep.astype(f32) * jnp.exp2(power_keep - power)
    values += other.astype(f32) * jnp.exp2(power_other - power)
    marked = lax.broadcasted_iota(i32, keep.shape, 1) >= depth
    whole = jnp.where(marked, power, jnp.round(values)).astype(i16)
    even = [whole] + [swap(whole, away) for away in range(2, shards, 2)]
    even, pair, timesteps = fence((even, pair, timesteps))

    even, pair = jnp.stack(even), jnp.stack(pair)
    odd = swap(even, 1)
    phase = (timesteps.astype(f32) / 1000.0 + 0.008) / 1.008 * (math.pi / 2)
    weight = jnp.sin(phase) * (1 / math.sqrt(channels * width))
    sums = score_products(even, trained, 0, 10**10)
    pair, sums = fence((pair, sums))
    found = [pair] + [swap(pair, away) for away in range(2, groups, 2)]
    odd, sums, weight = fence((odd, sums, weight))

    sums = sums + score_products(odd, trained, 1, 10**3)
    found = jnp.concatenate(found)
    terms = [sums]
    terms += [flip(terms[0], away) for away in range(factor - 1, 0, -1)][::-1]
    rows_found = [found[:, 0]] + [flip(found[:, away], away) for away in range(1, parts)]
    query_proj = output_rows(rows_found, groups, parts, own_rows, jump).reshape(channels, jump)
    terms, query_proj = fence((terms, query_proj))
    while len(terms) > 1:
        terms = [terms[at] + terms[at + 1] for at in range(0, len(terms), 2)]
    return (terms[0][:, 0] * weight, query_proj)


def solution(mesh):
    in_specs = (
        P("dp", None, None, None),
        P("dp", None, None, None),
        P("dp", None, None, None),
        P("dp", None, None, None),
        P("dp"),
        P("dp", "factor"),
        P(),
        P(None, "factor"),
    )
    out_specs = (P("dp"), P(None, "factor"))
    return jax.shard_map(
        on_device, mesh=mesh, in_specs=in_specs, out_specs=out_specs, check_vma=False
    )
```
